1024 devices in a mesh: row: 64 (over x, z), col: 16 (over y, core).
Axes of the slice: x: 8, y: 8, z: 8, core: 2. Of those that a mesh axis runs over, the one named last changes fastest.
Arguments:
- matrix: float32 [11, 8192, 2, 2048], P(None, 'row', None, 'col'), may hold values from 0 to 40, as said below
- panel: int32 [1], replicated, may hold values from 0 to 31
Outputs:
- trailing: float32 [11, 8192, 2, 2048], P(None, 'row', None, 'col')
- factor_panel: float32 [11, 8192, 128], P(None, 'row')
The draws below stay inside these ranges and needn't reach their ends.
Inputs may be any that keep to these rules, and one draw needn't show every extreme that they name: A[i, j] = w_i w_j k(x_i, x_j) for i != j and w_i^2 k(x_i, x_i) + s_i on the diagonal, with integer points x_i on a 64^3 grid, positive amplitudes w_i and nuggets s_i > 0, and k = 0.6 k_16 + 0.4 k_2 with k_l a Matern-3/2 kernel of length scale l (positive definite); so the matrix is symmetric where rows and columns coincide and every diagonal tile of the window is positive definite.
All inputs are finite; a program needn't handle non-finite values.
Results may differ from the reference program's by a relative error of at most 0.000088.
Values sent between devices are 32-bit elements; how exact they have to be, the bound alone decides.
No kernel may reach another device: no remote copies, remote signals or barrier semaphores. Data moves between devices by JAX's collectives and lax.ppermute only.
A program may use at most 32 MiB of HBM per device.

```python
import math
import jax
import jax.numpy as jnp
from jax import lax

N = 90112
NB = 128
CT_DEV = 2
RT = 11
WCOL = 4096
N_ROW = 64
N_COL = 16


def matern_term(dist, length_scale):
    scaled = math.sqrt(3.0) * dist / length_scale
    return (1.0 + scaled) * jnp.exp(-scaled)


def draw_matrix(key, part):
    key = jax.random.fold_in(key, 11)
    key_points, key_amp, key_nugget = jax.random.split(key, 3)
    points = jax.random.randint(key_points, (N, 3), 0, 64).astype(jnp.float32)
    amplitude = jnp.exp(jax.random.uniform(key_amp, (N,), jnp.float32, 0.0, math.log(3.2)))
    nugget = amplitude * amplitude * jnp.exp(jax.random.uniform(key_nugget, (N,), jnp.float32, math.log(0.25), 0.0))
    width_cols = CT_DEV * N_COL * NB
    squared = jnp.zeros((N, width_cols), jnp.float32)
    for axis_index in range(3):
        coord = points[:, axis_index]
        squared = squared + (coord[:, None] - coord[None, :width_cols]) ** 2
    dist = jnp.sqrt(squared)
    kernel = 0.6 * matern_term(dist, 16.0) + 0.4 * matern_term(dist, 2.0)
    values = amplitude[:, None] * amplitude[None, :width_cols] * kernel
    same = jnp.arange(N)[:, None] == jnp.arange(width_cols)[None, :]
    values = values + jnp.where(same, nugget[:, None], 0.0)
    return values.reshape(N // (NB * N_ROW), N_ROW * NB, CT_DEV, N_COL * NB).astype(jnp.float32)


def setup_inputs(seed: int = 0) -> dict:
    arg_keys = jax.random.split(jax.random.key(seed), 3)
    return {
        "matrix": draw_matrix(jax.random.fold_in(arg_keys[2], 71), 0),
        "panel": jax.random.randint(arg_keys[1], (1,), 0, CT_DEV * N_COL).astype(jnp.int32),
    }


def reference(matrix, panel):
    whole = matrix.reshape(N, WCOL)
    pivot_tile = panel[0].astype(jnp.int32)
    start = (pivot_tile * NB).astype(jnp.int32)
    anchor = jnp.int32(0)
    diag_block = lax.dynamic_slice(whole, (start, start), (NB, NB))
    factor = jnp.tril(jnp.linalg.cholesky(diag_block))
    column = lax.dynamic_slice(whole, (anchor, start), (N, NB))
    solved = lax.linalg.triangular_solve(factor, column, left_side=False, lower=True, transpose_a=True)
    row_tile = (jnp.arange(N) // NB).astype(jnp.int32)
    placed = jnp.tile(factor, (N // NB, 1))
    panel_full = jnp.where((row_tile == pivot_tile)[:, None], placed, solved)
    update = jnp.dot(panel_full.astype(jnp.float32), panel_full[:WCOL].T.astype(jnp.float32), precision=lax.Precision.HIGHEST, preferred_element_type=jnp.float32)
    col_tile = (jnp.arange(WCOL) // NB).astype(jnp.int32)
    keep_mask = (row_tile != pivot_tile)[:, None] & (col_tile != pivot_tile)[None, :]
    trailing = jnp.where(keep_mask, whole - update, jnp.float32(0.0))
    return (trailing.reshape(matrix.shape), panel_full.reshape(RT, N_ROW * NB, NB))
```

```python
import jax
import jax.numpy as jnp
from jax import lax
from jax.sharding import PartitionSpec as P

HIGHEST = lax.Precision.HIGHEST
AXES = ("row", "col")
X, Z, Y, CORE = (128, 8), (16, 8), (2, 8), (1, 2)


def hop(value, axis, source, bit, count, both=False):
    stride, size = axis
    done = size - 2 * bit if bit * 2 < size else 0
    holders = {source ^ mask for mask in range(size) if mask & ~done == 0}
    pairs = []
    for device in range(count):
        place = device // stride % size
        if both or place in holders:
            pairs.append((device, device ^ (bit * stride)))
    return value + lax.ppermute(value, AXES, pairs)


def first_half(key, count):
    pivot = 2 * key
    x, y = pivot // 8, pivot % 16 // 2

    def branch(strip, column):
        column = hop(column, Y, y, 4, count)
        strip = hop(strip, X, x, 4, count)
        strip = hop(strip, X, x, 2, count)
        column = hop(column, Y, y, 2, count)
        strip = hop(strip, X, x, 1, count, both=True)
        return strip, column

    return branch


def second_half(key, count):
    pivot = key
    z, y = pivot % 8, pivot % 16 // 2

    def branch(strip, column, at_col, which):
        column = hop(column, Y, y, 1, count, both=True)
        strip = hop(strip, Z, z, 4, count)
        strip = hop(strip, Z, z, 2, count)
        strip = hop(strip, Z, z, 1, count, both=True)
        column = hop(column, CORE, 0, 1, count, both=True)
        diag = jnp.where(at_col, lax.dynamic_index_in_dim(strip, which, 0, keepdims=False), 0.0)
        diag = hop(diag, Y, y, 4, count)
        diag = hop(diag, Y, y, 2, count)
        diag = hop(diag, Y, y, 1, count, both=True)
        return diag, strip, column

    return branch


def on_device(matrix, panel):
    rows_here, tile, cols_here, _ = matrix.shape
    row_count = lax.axis_size("row")
    col_count = lax.axis_size("col")
    count = row_count * col_count
    my_row = lax.axis_index("row")
    my_col = lax.axis_index("col")
    pivot = panel[0]
    which = pivot // col_count
    at_row = my_row == pivot
    at_col = my_col == pivot % col_count
    strip = jnp.where(at_row, jnp.swapaxes(matrix[0], 0, 1), 0.0)
    column = lax.dynamic_index_in_dim(matrix, which, 2, keepdims=False)
    column = jnp.where(at_col, column, 0.0)
    strip, column = lax.switch(
        pivot // 2, [first_half(k, count) for k in range(16)], strip, column
    )
    diag, strip, column = lax.switch(
        pivot % 16, [second_half(k, count) for k in range(16)], strip, column, at_col, which
    )
    split = [(2 * d, 2 * d + 1) for d in range(count // 2)]
    diag = lax.dynamic_index_in_dim(
        lax.all_gather(diag, "col", axis_index_groups=[[2 * d, 2 * d + 1] for d in range(8)]),
        pivot % 2, 0, keepdims=False,
    )
    factor = jnp.tril(jnp.linalg.cholesky(diag))
    inverse = lax.linalg.triangular_solve(
        factor, jnp.eye(tile, dtype=jnp.float32), left_side=True, lower=True
    )
    solved = jnp.einsum("aik,jk->aij", column, inverse, precision=HIGHEST)
    right = jnp.einsum("ik,ckj->cij", inverse, strip, precision=HIGHEST)
    tile_ids = jnp.arange(rows_here, dtype=jnp.int32) * row_count + my_row
    panel_rows = jnp.where((tile_ids == pivot)[:, None, None], factor[None], solved)
    update = jnp.einsum("aik,ckj->aicj", solved, right, precision=HIGHEST)
    col_ids = jnp.arange(cols_here, dtype=jnp.int32) * col_count + my_col
    keep = (tile_ids != pivot)[:, None, None, None] & (col_ids != pivot)[None, None, :, None]
    trailing = jnp.where(keep, matrix - update, jnp.float32(0.0))
    return (trailing, panel_rows)


def solution(mesh):
    placed = (P(None, "row", None, "col"), P())
    return jax.shard_map(
        on_device,
        mesh=mesh,
        in_specs=placed,
        out_specs=(P(None, "row", None, "col"), P(None, "row", None)),
        check_vma=False,
    )
```

```python
import jax
import jax.numpy as jnp
from jax import lax
from jax.sharding import PartitionSpec as P

HIGHEST = lax.Precision.HIGHEST
AXES = ("row", "col")
X, Z, Y = 128, 16, 2
RING = 8
COUNT = 1024


def shift(value, stride, step):
    pairs = []
    for device in range(COUNT):
        place = device // stride % RING
        pairs.append((device, device + ((place + step) % RING - place) * stride))
    return lax.ppermute(value, AXES, pairs)


def swap_cores(value):
    return lax.ppermute(value, AXES, [(d, d ^ 1) for d in range(COUNT)])


def spread(value, stride, at_source):
    first = value + shift(value, stride, 3) + shift(value, stride, -2)
    outer = jnp.where(at_source, 0.0, first)
    return first + shift(first, stride, 1) + shift(outer, stride, -1)


def after(value, earlier):
    return lax.optimization_barrier((value, earlier))[0]


def on_device(matrix, panel):
    rows_here, tile, cols_here, _ = matrix.shape
    row_count = lax.axis_size("row")
    col_count = lax.axis_size("col")
    my_row = lax.axis_index("row")
    my_col = lax.axis_index("col")
    pivot = panel[0]
    which = pivot // col_count
    pivot_col = pivot % col_count
    at_row = my_row == pivot
    at_col = my_col == pivot_col
    core = my_col % 2
    at_x = my_row // RING == pivot // RING
    at_z = my_row % RING == pivot % RING
    at_y = my_col // 2 == pivot_col // 2

    tiles = jnp.swapaxes(matrix[0], 0, 1)
    strip = jnp.where(at_row, tiles, 0.0)
    diag = jnp.where(at_col, lax.dynamic_index_in_dim(strip, which, 0, keepdims=False), 0.0)
    half = rows_here * tile // 2
    column = lax.dynamic_index_in_dim(matrix, which, 2, keepdims=False)
    column = jnp.where(at_col, column, 0.0).reshape(2, half, tile)

    diag = spread(diag, Y, at_y)
    strip = spread(strip, X, at_x)
    mine = lax.dynamic_index_in_dim(column, core, 0, keepdims=False)
    theirs = lax.dynamic_index_in_dim(column, 1 - core, 0, keepdims=False)
    mine = mine + swap_cores(theirs)

    mine = after(mine, diag)
    mine = spread(mine, Y, at_y)
    diag = diag + swap_cores(diag)
    strip = spread(after(strip, diag), Z, at_z)
    diag = spread(diag, X, at_x)
    diag = spread(diag, Z, at_z)
    theirs = swap_cores(mine)
    low = jnp.where(core == 0, mine, theirs)
    high = jnp.where(core == 0, theirs, mine)
    column = jnp.concatenate([low, high]).reshape(rows_here, tile, tile)

    factor = jnp.tril(jnp.linalg.cholesky(diag))
    inverse = lax.linalg.triangular_solve(
        factor, jnp.eye(tile, dtype=jnp.float32), left_side=True, lower=True
    )
    solved = jnp.einsum("aik,jk->aij", column, inverse, precision=HIGHEST)
    right = jnp.einsum("ik,ckj->cij", inverse, strip, precision=HIGHEST)
    tile_ids = jnp.arange(rows_here, dtype=jnp.int32) * row_count + my_row
    panel_rows = jnp.where((tile_ids == pivot)[:, None, None], factor[None], solved)
    update = jnp.einsum("aik,ckj->aicj", solved, right, precision=HIGHEST)
    col_ids = jnp.arange(cols_here, dtype=jnp.int32) * col_count + my_col
    keep = (tile_ids != pivot)[:, None, None, None] & (col_ids != pivot)[None, None, :, None]
    trailing = jnp.where(keep, matrix - update, jnp.float32(0.0))
    return (trailing, panel_rows)


def solution(mesh):
    placed = (P(None, "row", None, "col"), P())
    return jax.shard_map(
        on_device,
        mesh=mesh,
        in_specs=placed,
        out_specs=(P(None, "row", None, "col"), P(None, "row", None)),
        check_vma=False,
    )
```

```python
import jax
import jax.numpy as jnp
from jax import lax
from jax.sharding import PartitionSpec as P

HIGHEST = lax.Precision.HIGHEST
AXES = ("row", "col")
X, Z, Y = 128, 16, 2
RING = 8
COUNT = 1024


def swap_cores(value):
    return lax.ppermute(value, AXES, [(d, d ^ 1) for d in range(COUNT)])


def hop(value, stride, source, step):
    half = source & 4
    if step == 0:
        moves = {source: source ^ 2, source ^ 4: source ^ 6}
    elif step == 1:
        moves = {p: 6 - p if p % 2 == 0 else 8 - p for p in range(RING) if p & 4 == half and p % 2 == source % 2}
    else:
        moves = {p: p ^ 1 for p in range(RING) if p % 2 == source % 2}
    pairs = []
    for device in range(COUNT):
        place = device // stride % RING
        if place in moves:
            pairs.append((device, device + (moves[place] - place) * stride))
    return value + lax.ppermute(value, AXES, pairs)


def after(value, earlier):
    return lax.optimization_barrier((value, earlier))[0]


def along_x(key):
    x, y = key // 4, key % 8

    def branch(strip, mine, theirs):
        mine = mine + swap_cores(theirs)
        strip = hop(strip, X, x, 0)
        mine = hop(after(mine, strip), Y, y, 0)
        strip = hop(strip, X, x, 1)
        strip = hop(strip, X, x, 2)
        return strip, mine

    return branch


def along_z(key):
    z, y = key % 8, key // 2

    def branch(strip, mine):
        mine = hop(mine, Y, y, 1)
        for step in range(3):
            strip = hop(strip, Z, z, step)
        return strip, mine

    return branch


def along_y(key):
    y = key

    def branch(diag, mine):
        for step in range(3):
            diag = hop(diag, Y, y, step)
        mine = hop(mine, Y, y, 2)
        return diag, mine

    return branch


def on_device(matrix, panel):
    rows_here, tile, cols_here, _ = matrix.shape
    row_count = lax.axis_size("row")
    col_count = lax.axis_size("col")
    my_row = lax.axis_index("row")
    my_col = lax.axis_index("col")
    pivot = panel[0]
    which = pivot // col_count
    pivot_col = pivot % col_count
    at_row = my_row == pivot
    at_col = my_col == pivot_col
    core = my_col % 2

    tiles = jnp.swapaxes(matrix[0], 0, 1)
    strip = jnp.where(at_row, tiles, 0.0)
    half = rows_here * tile // 2
    column = lax.dynamic_index_in_dim(matrix, which, 2, keepdims=False)
    column = jnp.where(at_col, column, 0.0).reshape(2, half, tile)
    mine = lax.dynamic_index_in_dim(column, core, 0, keepdims=False)
    theirs = lax.dynamic_index_in_dim(column, 1 - core, 0, keepdims=False)

    strip, mine = lax.switch(pivot // 2, [along_x(k) for k in range(16)], strip, mine, theirs)
    strip, mine = lax.switch(pivot % 16, [along_z(k) for k in range(16)], strip, mine)
    diag = jnp.where(at_col, lax.dynamic_index_in_dim(strip, which, 0, keepdims=False), 0.0)
    diag, mine = lax.switch(pivot % 16 // 2, [along_y(k) for k in range(8)], diag, mine)
    diag = diag + swap_cores(diag)
    theirs = swap_cores(mine)
    low = jnp.where(core == 0, mine, theirs)
    high = jnp.where(core == 0, theirs, mine)
    column = jnp.concatenate([low, high]).reshape(rows_here, tile, tile)

    factor = jnp.tril(jnp.linalg.cholesky(diag))
    inverse = lax.linalg.triangular_solve(
        factor, jnp.eye(tile, dtype=jnp.float32), left_side=True, lower=True
    )
    solved = jnp.einsum("aik,jk->aij", column, inverse, precision=HIGHEST)
    right = jnp.einsum("ik,ckj->cij", inverse, strip, precision=HIGHEST)
    tile_ids = jnp.arange(rows_here, dtype=jnp.int32) * row_count + my_row
    panel_rows = jnp.where((tile_ids == pivot)[:, None, None], factor[None], solved)
    update = jnp.einsum("aik,ckj->aicj", solved, right, precision=HIGHEST)
    col_ids = jnp.arange(cols_here, dtype=jnp.int32) * col_count + my_col
    keep = (tile_ids != pivot)[:, None, None, None] & (col_ids != pivot)[None, None, :, None]
    trailing = jnp.where(keep, matrix - update, jnp.float32(0.0))
    return (trailing, panel_rows)


def solution(mesh):
    placed = (P(None, "row", None, "col"), P())
    return jax.shard_map(
        on_device,
        mesh=mesh,
        in_specs=placed,
        out_specs=(P(None, "row", None, "col"), P(None, "row", None)),
        check_vma=False,
    )
```

```python
import functools

import jax
import jax.numpy as jnp
from jax import lax
from jax.experimental import pallas as pl
from jax.experimental.pallas import tpu as pltpu
from jax.sharding import PartitionSpec as P

HIGHEST = lax.Precision.HIGHEST
AXES = ("row", "col")
X, Z, Y = 128, 16, 2
RING = 8
COUNT = 1024
TILE = 128
BLOCK = 16


def swap_cores(value):
    return lax.ppermute(value, AXES, [(d, d ^ 1) for d in range(COUNT)])


def hop(value, stride, source, step, core=None):
    same = [p for p in range(RING) if p % 2 == source % 2]
    if step == 0:
        moves = {source: source ^ 2, source ^ 4: source ^ 6}
    elif step == 1:
        held = same if core is not None else [p for p in same if p & 4 == source & 4]
        moves = {p: 6 - p if p % 2 == 0 else 8 - p for p in held}
    else:
        moves = {p: p ^ 1 for p in (same if core is None else range(RING))}
    pairs = []
    for device in range(COUNT):
        place = device // stride % RING
        if place in moves and core in (None, device % 2):
            pairs.append((device, device + (moves[place] - place) * stride))
    return value + lax.ppermute(value, AXES, pairs)


def after(value, earlier):
    return lax.optimization_barrier((value, earlier))[0]


def along_x(key):
    x, y, core = key // 8, key % 16 // 2, key % 2

    def branch(strip, column):
        strip = hop(strip, X, x, 0)
        column = hop(after(column, strip), Y, y, 0, core)
        strip = hop(strip, X, x, 1)
        strip = hop(strip, X, x, 2)
        return strip, column

    return branch


def along_z(key):
    z, y, core = key, key // 2, key % 2

    def branch(strip, column):
        column = hop(column, Y, y, 1, core)
        for step in range(3):
            strip = hop(strip, Z, z, step)
        return strip, column

    return branch


def along_y(key):
    y, core = key // 2, key % 2

    def branch(diag, column):
        for step in range(3):
            diag = hop(diag, Y, y, step, core)
        column = hop(column, Y, y, 2, core)
        return diag, column

    return branch


def row_of(value, row):
    return jnp.broadcast_to(value[row : row + 1, :], value.shape)


def factor_kernel(diag_ref, factor_ref, inverse_ref, left_ref, right_ref):
    sub = lax.broadcasted_iota(jnp.int32, (BLOCK, TILE), 0)
    lane = lax.broadcasted_iota(jnp.int32, (TILE, TILE), 1)
    row = lax.broadcasted_iota(jnp.int32, (TILE, TILE), 0)
    left_ref[...] = diag_ref[...]
    right_ref[...] = jnp.where(lane == row, 1.0, 0.0)
    for start in range(0, TILE, BLOCK):
        stop = start + BLOCK
        rows = pl.ds(start, BLOCK)
        left, right = left_ref[rows, :], right_ref[rows, :]
        cols = [jnp.broadcast_to(left[:, i : i + 1], (BLOCK, TILE)) for i in range(start, stop)]
        pivots = jnp.ones((BLOCK, TILE), jnp.float32)
        for j in range(BLOCK):
            pivot = row_of(cols[j], j)
            pivots = jnp.where(sub == j, pivot, pivots)
            scale = jnp.where(sub > j, cols[j], 0.0) * (1.0 / pivot)
            for i in range(j + 1, BLOCK):
                cols[i] = cols[i] - scale * row_of(cols[i], j)
            left = left - scale * row_of(left, j)
            right = right - scale * row_of(right, j)
        root = lax.rsqrt(pivots)
        root = root * (1.5 - 0.5 * pivots * root * root)
        left, right = left * root, right * root
        left_ref[rows, :] = left
        right_ref[rows, :] = right
        if stop < TILE:
            rest = pl.ds(stop, TILE - stop)
            step = lax.dot_general(
                left[:, stop:], jnp.concatenate([left, right], axis=1), (((0,), (0,)), ((), ())),
                precision=HIGHEST, preferred_element_type=jnp.float32,
            )
            left_ref[rest, :] = left_ref[rest, :] - step[:, :TILE]
            right_ref[rest, :] = right_ref[rest, :] - step[:, TILE:]
    factor_ref[...] = jnp.where(lane <= row, left_ref[...].T, 0.0)
    inverse_ref[...] = jnp.where(lane <= row, right_ref[...], 0.0)


def factorize(diag):
    shape = jax.ShapeDtypeStruct((TILE, TILE), jnp.float32)
    spec = pl.BlockSpec(memory_space=pltpu.VMEM)
    return pl.pallas_call(
        factor_kernel,
        out_shape=(shape, shape),
        in_specs=[spec],
        out_specs=(spec, spec),
        scratch_shapes=[pltpu.VMEM((TILE, TILE), jnp.float32)] * 2,
    )(diag)


def update_kernel(
    row_count, col_count, place_ref, factor_ref, inverse_ref, strip_ref, mine_ref, theirs_ref, matrix_ref,
    trailing_ref, panel_ref, out, solved, out_sems, solved_sems,
):
    tiles, cols = mine_ref.shape[0], strip_ref.shape[0]
    pivot, my_row, my_col = place_ref[0], place_ref[1], place_ref[2]
    inverse = inverse_ref[...]
    strip = jnp.concatenate([strip_ref[k] for k in range(cols)], axis=1)
    right = jnp.dot(inverse, strip, precision=HIGHEST, preferred_element_type=jnp.float32)
    copies = []
    for a in range(tiles):
        is_pivot = a * row_count + my_row == pivot
        column = mine_ref[a] + theirs_ref[a]
        left = lax.dot_general(
            column, inverse, (((1,), (1,)), ((), ())), precision=HIGHEST, preferred_element_type=jnp.float32
        )
        solved[a] = jnp.where(is_pivot, factor_ref[...], left)
        copies.append(pltpu.make_async_copy(solved.at[a], panel_ref.at[a], solved_sems.at[a]))
        copies[-1].start()
        step = jnp.dot(left, right, precision=HIGHEST, preferred_element_type=jnp.float32)
        for k in range(cols):
            zero = is_pivot | (k * col_count + my_col == pivot)
            rows = pl.ds(a * TILE * cols + k, TILE, stride=cols)
            kept = matrix_ref[rows, :] - step[:, k * TILE : (k + 1) * TILE]
            out[rows, :] = jnp.where(zero, 0.0, kept)
        block = pl.ds(a * TILE * cols, TILE * cols)
        copies.append(pltpu.make_async_copy(out.at[block], trailing_ref.at[block], out_sems.at[a]))
        copies[-1].start()
    for copy in copies:
        copy.wait()


def update(place, factor, inverse, strip, mine, theirs, matrix, row_count, col_count):
    tiles = mine.shape[0]
    vmem = pl.BlockSpec(memory_space=pltpu.VMEM)
    hbm = pl.BlockSpec(memory_space=pl.ANY)
    return pl.pallas_call(
        functools.partial(update_kernel, row_count, col_count),
        out_shape=(
            jax.ShapeDtypeStruct(matrix.shape, jnp.float32),
            jax.ShapeDtypeStruct(mine.shape, jnp.float32),
        ),
        in_specs=[pl.BlockSpec(memory_space=pltpu.SMEM)] + [vmem] * 6,
        out_specs=(hbm, hbm),
        scratch_shapes=[
            pltpu.VMEM(matrix.shape, jnp.float32),
            pltpu.VMEM(mine.shape, jnp.float32),
            pltpu.SemaphoreType.DMA((tiles,)),
            pltpu.SemaphoreType.DMA((tiles,)),
        ],
        compiler_params=pltpu.CompilerParams(vmem_limit_bytes=24 * 2**20),
    )(place, factor, inverse, strip, mine, theirs, matrix)


def on_device(matrix, panel):
    rows_here, tile, cols_here, _ = matrix.shape
    row_count = lax.axis_size("row")
    col_count = lax.axis_size("col")
    my_row = lax.axis_index("row")
    my_col = lax.axis_index("col")
    pivot = panel[0]
    which = pivot // col_count
    at_row = my_row == pivot
    at_col = my_col == pivot % col_count

    strip = jnp.where(at_row, jnp.swapaxes(matrix[0], 0, 1), 0.0)
    column = jnp.where(at_col, lax.dynamic_index_in_dim(matrix, which, 2, keepdims=False), 0.0)
    strip, column = lax.switch(pivot, [along_x(k) for k in range(32)], strip, column)
    strip, column = lax.switch(pivot % 8, [along_z(k) for k in range(8)], strip, column)
    diag = jnp.where(at_col, lax.dynamic_index_in_dim(strip, which, 0, keepdims=False), 0.0)
    diag, column = lax.switch(pivot % 8, [along_y(k) for k in range(8)], diag, column)
    diag = diag + swap_cores(diag)
    theirs = swap_cores(after(column, diag))

    factor, inverse = factorize(diag)
    place = jnp.stack([pivot, my_row, my_col])
    flat = matrix.reshape(rows_here * tile * cols_here, tile)
    trailing, panel_rows = update(
        place, factor, inverse, strip, column, theirs, flat, row_count, col_count
    )
    return trailing.reshape(matrix.shape), panel_rows


def solution(mesh):
    placed = (P(None, "row", None, "col"), P())
    return jax.shard_map(
        on_device,
        mesh=mesh,
        in_specs=placed,
        out_specs=(P(None, "row", None, "col"), P(None, "row", None)),
        check_vma=False,
    )
```

```python
import functools

import jax
import jax.numpy as jnp
from jax import lax
from jax.experimental import pallas as pl
from jax.experimental.pallas import tpu as pltpu
from jax.sharding import PartitionSpec as P

HIGHEST = lax.Precision.HIGHEST
AXES = ("row", "col")
X, Z, Y = 128, 16, 2
RING = 8
COUNT = 1024
TILE = 128
BLOCK = 16


def swap_cores(value):
    return lax.ppermute(value, AXES, [(d, d ^ 1) for d in range(COUNT)])


def hop(value, stride, source, step, core=None):
    same = [p for p in range(RING) if p % 2 == source % 2]
    if step == 0:
        moves = {source: source ^ 2, source ^ 4: source ^ 6}
    elif step == 1:
        held = same if core is not None else [p for p in same if p & 4 == source & 4]
        moves = {p: 6 - p if p % 2 == 0 else 8 - p for p in held}
    else:
        moves = {p: p ^ 1 for p in same}
    pairs = []
    for device in range(COUNT):
        place = device // stride % RING
        if place in moves and core in (None, device % 2):
            pairs.append((device, device + (moves[place] - place) * stride))
    return value + lax.ppermute(value, AXES, pairs)


def after(value, earlier):
    return lax.optimization_barrier((value, earlier))[0]


def along_xz(pivot):
    x, z, y, core = pivot // 8, pivot % 8, pivot % 16 // 2, pivot % 2

    def branch(strip, column):
        strip = hop(strip, X, x, 0)
        column = hop(column, Y, y, 0, core)
        strip = hop(strip, X, x, 1)
        column = hop(after(column, strip), Y, y, 1, core)
        strip = hop(strip, X, x, 2)
        strip = hop(strip, Z, z, 0)
        column = hop(after(column, strip), Y, y, 2, core)
        strip = hop(strip, Z, z, 1)
        strip = hop(strip, Z, z, 2)
        return strip, column

    return branch


def along_y(key):
    y, core = key // 2, key % 2

    def branch(diag):
        for step in range(3):
            diag = hop(diag, Y, y, step, core)
        return diag

    return branch


def cut_kernel(cols, place_ref, matrix_ref, strip_ref, column_ref):
    which, at_row, at_col = place_ref[0], place_ref[1] == 1, place_ref[2] == 1
    for k in range(cols):
        strip_ref[k] = jnp.where(at_row, matrix_ref[pl.ds(k, TILE, stride=cols), :], 0.0)
    for a in range(column_ref.shape[0]):
        rows = matrix_ref[pl.ds(a * TILE * cols + which, TILE, stride=cols), :]
        column_ref[a] = jnp.where(at_col, rows, 0.0)


def cut(place, matrix, tiles, cols):
    vmem = pl.BlockSpec(memory_space=pltpu.VMEM)
    return pl.pallas_call(
        functools.partial(cut_kernel, cols),
        out_shape=(
            jax.ShapeDtypeStruct((cols, TILE, TILE), jnp.float32),
            jax.ShapeDtypeStruct((tiles, TILE, TILE), jnp.float32),
        ),
        in_specs=[pl.BlockSpec(memory_space=pltpu.SMEM), vmem],
        out_specs=(vmem, vmem),
        compiler_params=pltpu.CompilerParams(vmem_limit_bytes=16 * 2**20),
    )(place, matrix)


def row_of(value, row):
    return jnp.broadcast_to(value[row : row + 1, :], value.shape)


def factor_kernel(diag_ref, factor_ref, inverse_ref, left_ref, right_ref):
    sub = lax.broadcasted_iota(jnp.int32, (BLOCK, TILE), 0)
    lane = lax.broadcasted_iota(jnp.int32, (TILE, TILE), 1)
    row = lax.broadcasted_iota(jnp.int32, (TILE, TILE), 0)
    left_ref[...] = diag_ref[...]
    right_ref[...] = jnp.where(lane == row, 1.0, 0.0)
    for start in range(0, TILE, BLOCK):
        stop = start + BLOCK
        rows = pl.ds(start, BLOCK)
        left, right = left_ref[rows, :], right_ref[rows, :]
        cols = [jnp.broadcast_to(left[:, i : i + 1], (BLOCK, TILE)) for i in range(start, stop)]
        pivots = jnp.ones((BLOCK, TILE), jnp.float32)
        for j in range(BLOCK):
            pivot = row_of(cols[j], j)
            pivots = jnp.where(sub == j, pivot, pivots)
            scale = jnp.where(sub > j, cols[j], 0.0) * (1.0 / pivot)
            for i in range(j + 1, BLOCK):
                cols[i] = cols[i] - scale * row_of(cols[i], j)
            left = left - scale * row_of(left, j)
            right = right - scale * row_of(right, j)
        root = lax.rsqrt(pivots)
        root = root * (1.5 - 0.5 * pivots * root * root)
        left, right = left * root, right * root
        left_ref[rows, :] = left
        right_ref[rows, :] = right
        if stop < TILE:
            rest = pl.ds(stop, TILE - stop)
            step = lax.dot_general(
                left[:, stop:], jnp.concatenate([left, right], axis=1), (((0,), (0,)), ((), ())),
                precision=HIGHEST, preferred_element_type=jnp.float32,
            )
            left_ref[rest, :] = left_ref[rest, :] - step[:, :TILE]
            right_ref[rest, :] = right_ref[rest, :] - step[:, TILE:]
    factor_ref[...] = jnp.where(lane <= row, left_ref[...].T, 0.0)
    inverse_ref[...] = jnp.where(lane <= row, right_ref[...], 0.0)


def factorize(diag):
    shape = jax.ShapeDtypeStruct((TILE, TILE), jnp.float32)
    spec = pl.BlockSpec(memory_space=pltpu.VMEM)
    return pl.pallas_call(
        factor_kernel,
        out_shape=(shape, shape),
        in_specs=[spec],
        out_specs=(spec, spec),
        scratch_shapes=[pltpu.VMEM((TILE, TILE), jnp.float32)] * 2,
    )(diag)


def update_kernel(
    row_count, col_count, place_ref, factor_ref, inverse_ref, strip_ref, mine_ref, theirs_ref, matrix_ref,
    trailing_ref, panel_ref, mine, theirs, out, solved, mine_sems, theirs_sems, out_sems, solved_sems,
):
    tiles, cols = mine_ref.shape[0], strip_ref.shape[0]
    fetches = []
    for a in range(tiles):
        fetches.append(pltpu.make_async_copy(mine_ref.at[a], mine.at[a], mine_sems.at[a]))
        fetches.append(pltpu.make_async_copy(theirs_ref.at[a], theirs.at[a], theirs_sems.at[a]))
        fetches[-2].start()
        fetches[-1].start()
    pivot, my_row, my_col = place_ref[0], place_ref[1], place_ref[2]
    inverse = inverse_ref[...]
    strip = jnp.concatenate([strip_ref[k] for k in range(cols)], axis=1)
    right = jnp.dot(inverse, strip, precision=HIGHEST, preferred_element_type=jnp.float32)
    copies = []
    for a in range(tiles):
        is_pivot = a * row_count + my_row == pivot
        fetches[2 * a].wait()
        fetches[2 * a + 1].wait()
        column = mine[a] + theirs[a]
        left = lax.dot_general(
            column, inverse, (((1,), (1,)), ((), ())), precision=HIGHEST, preferred_element_type=jnp.float32
        )
        solved[a] = jnp.where(is_pivot, factor_ref[...], left)
        copies.append(pltpu.make_async_copy(solved.at[a], panel_ref.at[a], solved_sems.at[a]))
        copies[-1].start()
        step = jnp.dot(left, right, precision=HIGHEST, preferred_element_type=jnp.float32)
        for k in range(cols):
            zero = is_pivot | (k * col_count + my_col == pivot)
            rows = pl.ds(a * TILE * cols + k, TILE, stride=cols)
            kept = matrix_ref[rows, :] - step[:, k * TILE : (k + 1) * TILE]
            out[rows, :] = jnp.where(zero, 0.0, kept)
        block = pl.ds(a * TILE * cols, TILE * cols)
        copies.append(pltpu.make_async_copy(out.at[block], trailing_ref.at[block], out_sems.at[a]))
        copies[-1].start()
    for copy in copies:
        copy.wait()


def update(place, factor, inverse, strip, mine, theirs, matrix, row_count, col_count):
    tiles = mine.shape[0]
    vmem = pl.BlockSpec(memory_space=pltpu.VMEM)
    hbm = pl.BlockSpec(memory_space=pl.ANY)
    return pl.pallas_call(
        functools.partial(update_kernel, row_count, col_count),
        out_shape=(
            jax.ShapeDtypeStruct(matrix.shape, jnp.float32),
            jax.ShapeDtypeStruct(mine.shape, jnp.float32),
        ),
        in_specs=[pl.BlockSpec(memory_space=pltpu.SMEM), vmem, vmem, vmem, hbm, hbm, vmem],
        out_specs=(hbm, hbm),
        scratch_shapes=[
            pltpu.VMEM(mine.shape, jnp.float32),
            pltpu.VMEM(mine.shape, jnp.float32),
            pltpu.VMEM(matrix.shape, jnp.float32),
            pltpu.VMEM(mine.shape, jnp.float32),
        ]
        + [pltpu.SemaphoreType.DMA((tiles,))] * 4,
        compiler_params=pltpu.CompilerParams(vmem_limit_bytes=24 * 2**20),
    )(place, factor, inverse, strip, mine, theirs, matrix)


def on_device(matrix, panel):
    rows_here, tile, cols_here, _ = matrix.shape
    row_count = lax.axis_size("row")
    col_count = lax.axis_size("col")
    my_row = lax.axis_index("row")
    my_col = lax.axis_index("col")
    pivot = panel[0]
    which = pivot // col_count
    at_row = my_row == pivot
    at_col = my_col == pivot % col_count

    flat = matrix.reshape(rows_here * tile * cols_here, tile)
    held = jnp.stack([which, at_row.astype(jnp.int32), at_col.astype(jnp.int32)])
    strip, column = cut(held, flat, rows_here, cols_here)
    pivots = cols_here * col_count
    strip, column = lax.switch(
        pivot, [along_xz(p) for p in range(pivots)], strip, column
    )
    diag = jnp.where(at_col, lax.dynamic_index_in_dim(strip, which, 0, keepdims=False), 0.0)
    diag = lax.switch(pivot % 8, [along_y(k) for k in range(8)], diag)
    diag = diag + swap_cores(diag)
    theirs = swap_cores(after(column, diag))

    factor, inverse = factorize(diag)
    place = jnp.stack([pivot, my_row, my_col])
    trailing, panel_rows = update(
        place, factor, inverse, strip, column, theirs, flat, row_count, col_count
    )
    return trailing.reshape(matrix.shape), panel_rows


def solution(mesh):
    placed = (P(None, "row", None, "col"), P())
    return jax.shard_map(
        on_device,
        mesh=mesh,
        in_specs=placed,
        out_specs=(P(None, "row", None, "col"), P(None, "row", None)),
        check_vma=False,
    )
```

```python
import functools

import jax
import jax.numpy as jnp
from jax import lax
from jax.experimental import pallas as pl
from jax.experimental.pallas import tpu as pltpu
from jax.sharding import PartitionSpec as P

HIGHEST = lax.Precision.HIGHEST
AXES = ("row", "col")
X, Z, Y = 128, 16, 2
RING = 8
COUNT = 1024
TILE = 128
BLOCK = 16


def swap_cores(value):
    return lax.ppermute(value, AXES, [(d, d ^ 1) for d in range(COUNT)])


def hop(value, stride, source, step, core=None):
    same = [p for p in range(RING) if p % 2 == source % 2]
    if step == 0:
        moves = {source: source ^ 2, source ^ 4: source ^ 6}
    elif step == 1:
        held = same if core is not None else [p for p in same if p & 4 == source & 4]
        moves = {p: 6 - p if p % 2 == 0 else 8 - p for p in held}
    else:
        moves = {p: p ^ 1 for p in (same if core is None else range(RING))}
    pairs = []
    for device in range(COUNT):
        place = device // stride % RING
        if place in moves and core in (None, device % 2):
            pairs.append((device, device + (moves[place] - place) * stride))
    return value + lax.ppermute(value, AXES, pairs)


def after(value, earlier):
    return lax.optimization_barrier((value, earlier))[0]


def along_x(pivot):
    x, y, core = pivot // 8, pivot % 16 // 2, pivot % 2

    def branch(strip, column):
        strip = hop(strip, X, x, 0)
        column = hop(after(column, strip), Y, y, 0, core)
        strip = hop(strip, X, x, 1)
        strip = hop(strip, X, x, 2)
        return strip, column

    return branch


def along_z(key):
    z, y, core = key, key // 2, key % 2

    def branch(strip, column):
        column = hop(column, Y, y, 1, core)
        for step in range(3):
            strip = hop(strip, Z, z, step)
        return strip, column

    return branch


def along_y(key):
    y, core = key // 2, key % 2

    def branch(diag, kept, given):
        received = swap_cores(given)
        diag = hop(diag, Y, y, 0, core)
        half = hop(kept + after(received, diag), Y, y, 2)
        diag = hop(diag, Y, y, 1, core)
        diag = hop(diag, Y, y, 2, core)
        return lax.optimization_barrier((diag, half))

    return branch


def cut_kernel(cols, place_ref, matrix_ref, strip_ref, column_ref):
    which, at_row, at_col = place_ref[0], place_ref[1] == 1, place_ref[2] == 1
    for k in range(cols):
        strip_ref[k] = jnp.where(at_row, matrix_ref[pl.ds(k, TILE, stride=cols), :], 0.0)
    for a in range(column_ref.shape[0]):
        rows = matrix_ref[pl.ds(a * TILE * cols + which, TILE, stride=cols), :]
        column_ref[a] = jnp.where(at_col, rows, 0.0)


def cut(place, matrix, tiles, cols):
    vmem = pl.BlockSpec(memory_space=pltpu.VMEM)
    return pl.pallas_call(
        functools.partial(cut_kernel, cols),
        out_shape=(
            jax.ShapeDtypeStruct((cols, TILE, TILE), jnp.float32),
            jax.ShapeDtypeStruct((tiles, TILE, TILE), jnp.float32),
        ),
        in_specs=[pl.BlockSpec(memory_space=pltpu.SMEM), vmem],
        out_specs=(vmem, vmem),
        compiler_params=pltpu.CompilerParams(vmem_limit_bytes=16 * 2**20),
    )(place, matrix)


def row_of(value, row):
    return jnp.broadcast_to(value[row : row + 1, :], value.shape)


def factor_kernel(diag_ref, factor_ref, inverse_ref, left_ref, right_ref):
    sub = lax.broadcasted_iota(jnp.int32, (BLOCK, TILE), 0)
    lane = lax.broadcasted_iota(jnp.int32, (TILE, TILE), 1)
    row = lax.broadcasted_iota(jnp.int32, (TILE, TILE), 0)
    left_ref[...] = diag_ref[...]
    right_ref[...] = jnp.where(lane == row, 1.0, 0.0)
    for start in range(0, TILE, BLOCK):
        stop = start + BLOCK
        rows = pl.ds(start, BLOCK)
        left, right = left_ref[rows, :], right_ref[rows, :]
        cols = [jnp.broadcast_to(left[:, i : i + 1], (BLOCK, TILE)) for i in range(start, stop)]
        pivots = jnp.ones((BLOCK, TILE), jnp.float32)
        for j in range(BLOCK):
            pivot = row_of(cols[j], j)
            pivots = jnp.where(sub == j, pivot, pivots)
            scale = jnp.where(sub > j, cols[j], 0.0) * (1.0 / pivot)
            for i in range(j + 1, BLOCK):
                cols[i] = cols[i] - scale * row_of(cols[i], j)
            left = left - scale * row_of(left, j)
            right = right - scale * row_of(right, j)
        root = lax.rsqrt(pivots)
        root = root * (1.5 - 0.5 * pivots * root * root)
        left, right = left * root, right * root
        left_ref[rows, :] = left
        right_ref[rows, :] = right
        if stop < TILE:
            rest = pl.ds(stop, TILE - stop)
            step = lax.dot_general(
                left[:, stop:], jnp.concatenate([left, right], axis=1), (((0,), (0,)), ((), ())),
                precision=HIGHEST, preferred_element_type=jnp.float32,
            )
            left_ref[rest, :] = left_ref[rest, :] - step[:, :TILE]
            right_ref[rest, :] = right_ref[rest, :] - step[:, TILE:]
    factor_ref[...] = jnp.where(lane <= row, left_ref[...].T, 0.0)
    inverse_ref[...] = jnp.where(lane <= row, right_ref[...], 0.0)


def factorize(diag):
    shape = jax.ShapeDtypeStruct((TILE, TILE), jnp.float32)
    spec = pl.BlockSpec(memory_space=pltpu.VMEM)
    return pl.pallas_call(
        factor_kernel,
        out_shape=(shape, shape),
        in_specs=[spec],
        out_specs=(spec, spec),
        scratch_shapes=[pltpu.VMEM((TILE, TILE), jnp.float32)] * 2,
    )(diag)


def update_kernel(
    row_count, col_count, place_ref, factor_ref, inverse_ref, strip_ref, mine_ref, theirs_ref, matrix_ref,
    trailing_ref, panel_ref, out, solved, out_sems, solved_sems,
):
    tiles, cols = solved.shape[0], strip_ref.shape[0]
    half = mine_ref.shape[0]
    pivot, my_row, my_col, core = place_ref[0], place_ref[1], place_ref[2], place_ref[3]
    inverse = inverse_ref[...]
    strip = jnp.concatenate([strip_ref[k] for k in range(cols)], axis=1)
    right = jnp.dot(inverse, strip, precision=HIGHEST, preferred_element_type=jnp.float32)
    copies = []
    for a in range(tiles):
        is_pivot = a * row_count + my_row == pivot
        low = a < half
        i = a if low else a - (tiles - half)
        column = jnp.where(core == (0 if low else 1), mine_ref[i], theirs_ref[i])
        left = lax.dot_general(
            column, inverse, (((1,), (1,)), ((), ())), precision=HIGHEST, preferred_element_type=jnp.float32
        )
        solved[a] = jnp.where(is_pivot, factor_ref[...], left)
        copies.append(pltpu.make_async_copy(solved.at[a], panel_ref.at[a], solved_sems.at[a]))
        copies[-1].start()
        step = jnp.dot(left, right, precision=HIGHEST, preferred_element_type=jnp.float32)
        for k in range(cols):
            zero = is_pivot | (k * col_count + my_col == pivot)
            rows = pl.ds(a * TILE * cols + k, TILE, stride=cols)
            kept = matrix_ref[rows, :] - step[:, k * TILE : (k + 1) * TILE]
            out[rows, :] = jnp.where(zero, 0.0, kept)
        block = pl.ds(a * TILE * cols, TILE * cols)
        copies.append(pltpu.make_async_copy(out.at[block], trailing_ref.at[block], out_sems.at[a]))
        copies[-1].start()
    for copy in copies:
        copy.wait()


def update(place, factor, inverse, strip, mine, theirs, matrix, tiles, row_count, col_count):
    vmem = pl.BlockSpec(memory_space=pltpu.VMEM)
    hbm = pl.BlockSpec(memory_space=pl.ANY)
    panel = jax.ShapeDtypeStruct((tiles, TILE, TILE), jnp.float32)
    return pl.pallas_call(
        functools.partial(update_kernel, row_count, col_count),
        out_shape=(jax.ShapeDtypeStruct(matrix.shape, jnp.float32), panel),
        in_specs=[pl.BlockSpec(memory_space=pltpu.SMEM)] + [vmem] * 6,
        out_specs=(hbm, hbm),
        scratch_shapes=[
            pltpu.VMEM(matrix.shape, jnp.float32),
            pltpu.VMEM(panel.shape, jnp.float32),
            pltpu.SemaphoreType.DMA((tiles,)),
            pltpu.SemaphoreType.DMA((tiles,)),
        ],
        compiler_params=pltpu.CompilerParams(vmem_limit_bytes=16 * 2**20),
    )(place, factor, inverse, strip, mine, theirs, matrix)


def on_device(matrix, panel):
    rows_here, tile, cols_here, _ = matrix.shape
    row_count = lax.axis_size("row")
    col_count = lax.axis_size("col")
    my_row = lax.axis_index("row")
    my_col = lax.axis_index("col")
    pivot = panel[0]
    which = pivot // col_count
    at_row = my_row == pivot
    at_col = my_col == pivot % col_count

    flat = matrix.reshape(rows_here * tile * cols_here, tile)
    held = jnp.stack([which, at_row.astype(jnp.int32), at_col.astype(jnp.int32)])
    strip, column = cut(held, flat, rows_here, cols_here)
    pivots = cols_here * col_count
    strip, column = lax.switch(pivot, [along_x(p) for p in range(pivots)], strip, column)
    strip, column = lax.switch(pivot % 8, [along_z(k) for k in range(8)], strip, column)
    diag = jnp.where(at_col, lax.dynamic_index_in_dim(strip, which, 0, keepdims=False), 0.0)
    core = my_col % 2
    half = (rows_here + 1) // 2
    kept = lax.dynamic_slice_in_dim(column, core * (rows_here - half), half)
    given = lax.dynamic_slice_in_dim(column, (1 - core) * (rows_here - half), half)
    diag, mine = lax.switch(pivot % 8, [along_y(k) for k in range(8)], diag, kept, given)
    diag = diag + swap_cores(diag)
    theirs = swap_cores(after(mine, diag))

    factor, inverse = factorize(diag)
    place = jnp.stack([pivot, my_row, my_col, core])
    trailing, panel_rows = update(
        place, factor, inverse, strip, mine, theirs, flat, rows_here, row_count, col_count
    )
    return trailing.reshape(matrix.shape), panel_rows


def solution(mesh):
    placed = (P(None, "row", None, "col"), P())
    return jax.shard_map(
        on_device,
        mesh=mesh,
        in_specs=placed,
        out_specs=(P(None, "row", None, "col"), P(None, "row", None)),
        check_vma=False,
    )
```

```python
import functools

import jax
import jax.numpy as jnp
from jax import lax
from jax.experimental import pallas as pl
from jax.experimental.pallas import tpu as pltpu
from jax.sharding import PartitionSpec as P

HIGHEST = lax.Precision.HIGHEST
AXES = ("row", "col")
X, Z, Y = 128, 16, 2
RING = 8
COUNT = 1024
TILE = 128
BLOCK = 16


def swap_cores(value):
    return lax.ppermute(value, AXES, [(d, d ^ 1) for d in range(COUNT)])


def hop(value, stride, source, step, core=None):
    same = [p for p in range(RING) if p % 2 == source % 2]
    if step == 0:
        moves = {source: source ^ 2, source ^ 4: source ^ 6}
    elif step == 1:
        held = same if core is not None else [p for p in same if p & 4 == source & 4]
        moves = {p: 6 - p if p % 2 == 0 else 8 - p for p in held}
    else:
        moves = {p: p ^ 1 for p in same}
    pairs = []
    for device in range(COUNT):
        place = device // stride % RING
        if place in moves and core in (None, device % 2):
            pairs.append((device, device + (moves[place] - place) * stride))
    return value + lax.ppermute(value, AXES, pairs)


def along_x(pivot):
    x, y, core = pivot // 8, pivot % 16 // 2, pivot % 2

    def branch(strip, column):
        strip = swap_cores(strip)
        column = hop(column, Y, y, 0, core)
        for step in range(3):
            strip = hop(strip, X, x, step)
        return lax.optimization_barrier((strip, column))

    return branch


def along_z(key):
    z, y, core = key, key // 2, key % 2

    def branch(strip, column):
        column = hop(column, Y, y, 1, core)
        for step in range(3):
            strip = hop(strip, Z, z, step)
        return lax.optimization_barrier((strip, column))

    return branch


def along_y(key):
    y, core = key // 2, key % 2

    def branch(diag, column):
        column = hop(column, Y, y, 2, core)
        for step in range(3):
            diag = hop(diag, Y, y, step, 1 - core)
        return lax.optimization_barrier((diag, column))

    return branch


def cut_kernel(cols, place_ref, matrix_ref, strip_ref, column_ref):
    which, at_row, at_col = place_ref[0], place_ref[1] == 1, place_ref[2] == 1
    for k in range(cols):
        strip_ref[k] = jnp.where(at_row, matrix_ref[pl.ds(k, TILE, stride=cols), :], 0.0)
    for a in range(column_ref.shape[0]):
        rows = matrix_ref[pl.ds(a * TILE * cols + which, TILE, stride=cols), :]
        column_ref[a] = jnp.where(at_col, rows, 0.0)


def cut(place, matrix, tiles, cols):
    vmem = pl.BlockSpec(memory_space=pltpu.VMEM)
    return pl.pallas_call(
        functools.partial(cut_kernel, cols),
        out_shape=(
            jax.ShapeDtypeStruct((cols, TILE, TILE), jnp.float32),
            jax.ShapeDtypeStruct((tiles, TILE, TILE), jnp.float32),
        ),
        in_specs=[pl.BlockSpec(memory_space=pltpu.SMEM), vmem],
        out_specs=(vmem, vmem),
        compiler_params=pltpu.CompilerParams(vmem_limit_bytes=16 * 2**20),
    )(place, matrix)


def row_of(value, row):
    return jnp.broadcast_to(value[row : row + 1, :], value.shape)


def factor_kernel(diag_ref, factor_ref, inverse_ref, left_ref, right_ref):
    sub = lax.broadcasted_iota(jnp.int32, (BLOCK, TILE), 0)
    lane = lax.broadcasted_iota(jnp.int32, (TILE, TILE), 1)
    row = lax.broadcasted_iota(jnp.int32, (TILE, TILE), 0)
    left_ref[...] = diag_ref[...]
    right_ref[...] = jnp.where(lane == row, 1.0, 0.0)
    for start in range(0, TILE, BLOCK):
        stop = start + BLOCK
        rows = pl.ds(start, BLOCK)
        left, right = left_ref[rows, :], right_ref[rows, :]
        cols = [jnp.broadcast_to(left[:, i : i + 1], (BLOCK, TILE)) for i in range(start, stop)]
        pivots = jnp.ones((BLOCK, TILE), jnp.float32)
        for j in range(BLOCK):
            pivot = row_of(cols[j], j)
            pivots = jnp.where(sub == j, pivot, pivots)
            scale = jnp.where(sub > j, cols[j], 0.0) * (1.0 / pivot)
            for i in range(j + 1, BLOCK):
                cols[i] = cols[i] - scale * row_of(cols[i], j)
            left = left - scale * row_of(left, j)
            right = right - scale * row_of(right, j)
        root = lax.rsqrt(pivots)
        root = root * (1.5 - 0.5 * pivots * root * root)
        left, right = left * root, right * root
        left_ref[rows, :] = left
        right_ref[rows, :] = right
        if stop < TILE:
            rest = pl.ds(stop, TILE - stop)
            step = lax.dot_general(
                left[:, stop:], jnp.concatenate([left, right], axis=1), (((0,), (0,)), ((), ())),
                precision=HIGHEST, preferred_element_type=jnp.float32,
            )
            left_ref[rest, :] = left_ref[rest, :] - step[:, :TILE]
            right_ref[rest, :] = right_ref[rest, :] - step[:, TILE:]
    factor_ref[...] = jnp.where(lane <= row, left_ref[...].T, 0.0)
    inverse_ref[...] = jnp.where(lane <= row, right_ref[...], 0.0)


def factorize(diag):
    shape = jax.ShapeDtypeStruct((TILE, TILE), jnp.float32)
    spec = pl.BlockSpec(memory_space=pltpu.VMEM)
    return pl.pallas_call(
        factor_kernel,
        out_shape=(shape, shape),
        in_specs=[spec],
        out_specs=(spec, spec),
        scratch_shapes=[pltpu.VMEM((TILE, TILE), jnp.float32)] * 2,
    )(diag)


def update_kernel(
    row_count, col_count, place_ref, factor_ref, inverse_ref, mine_ref, theirs_ref, matrix_ref, trailing_ref,
    panel_ref, out, solved, out_sems, solved_sems,
):
    tiles = solved.shape[0]
    cols = mine_ref.shape[0] - tiles
    pivot, my_row, my_col = place_ref[0], place_ref[1], place_ref[2]
    inverse = inverse_ref[...]
    strip = jnp.concatenate([theirs_ref[tiles + k] for k in range(cols)], axis=1)
    right = jnp.dot(inverse, strip, precision=HIGHEST, preferred_element_type=jnp.float32)
    copies = []
    for a in range(tiles):
        is_pivot = a * row_count + my_row == pivot
        column = mine_ref[a] + theirs_ref[a]
        left = lax.dot_general(
            column, inverse, (((1,), (1,)), ((), ())), precision=HIGHEST, preferred_element_type=jnp.float32
        )
        solved[a] = jnp.where(is_pivot, factor_ref[...], left)
        copies.append(pltpu.make_async_copy(solved.at[a], panel_ref.at[a], solved_sems.at[a]))
        copies[-1].start()
        step = jnp.dot(left, right, precision=HIGHEST, preferred_element_type=jnp.float32)
        for k in range(cols):
            zero = is_pivot | (k * col_count + my_col == pivot)
            rows = pl.ds(a * TILE * cols + k, TILE, stride=cols)
            kept = matrix_ref[rows, :] - step[:, k * TILE : (k + 1) * TILE]
            out[rows, :] = jnp.where(zero, 0.0, kept)
        block = pl.ds(a * TILE * cols, TILE * cols)
        copies.append(pltpu.make_async_copy(out.at[block], trailing_ref.at[block], out_sems.at[a]))
        copies[-1].start()
    for copy in copies:
        copy.wait()


def update(place, factor, inverse, mine, theirs, matrix, tiles, row_count, col_count):
    vmem = pl.BlockSpec(memory_space=pltpu.VMEM)
    hbm = pl.BlockSpec(memory_space=pl.ANY)
    panel = jax.ShapeDtypeStruct((tiles, TILE, TILE), jnp.float32)
    return pl.pallas_call(
        functools.partial(update_kernel, row_count, col_count),
        out_shape=(jax.ShapeDtypeStruct(matrix.shape, jnp.float32), panel),
        in_specs=[pl.BlockSpec(memory_space=pltpu.SMEM)] + [vmem] * 5,
        out_specs=(hbm, hbm),
        scratch_shapes=[
            pltpu.VMEM(matrix.shape, jnp.float32),
            pltpu.VMEM(panel.shape, jnp.float32),
            pltpu.SemaphoreType.DMA((tiles,)),
            pltpu.SemaphoreType.DMA((tiles,)),
        ],
        compiler_params=pltpu.CompilerParams(vmem_limit_bytes=16 * 2**20),
    )(place, factor, inverse, mine, theirs, matrix)


def on_device(matrix, panel):
    rows_here, tile, cols_here, _ = matrix.shape
    row_count = lax.axis_size("row")
    col_count = lax.axis_size("col")
    my_row = lax.axis_index("row")
    my_col = lax.axis_index("col")
    pivot = panel[0]
    which = pivot // col_count
    at_row = my_row == pivot
    at_col = my_col == pivot % col_count

    flat = matrix.reshape(rows_here * tile * cols_here, tile)
    held = jnp.stack([which, at_row.astype(jnp.int32), at_col.astype(jnp.int32)])
    strip, column = cut(held, flat, rows_here, cols_here)
    pivots = cols_here * col_count
    strip, column = lax.switch(pivot, [along_x(p) for p in range(pivots)], strip, column)
    strip, column = lax.switch(pivot % 8, [along_z(k) for k in range(8)], strip, column)
    crossed = my_col ^ 1 == pivot % col_count
    diag = jnp.where(crossed, lax.dynamic_index_in_dim(strip, which, 0, keepdims=False), 0.0)
    diag, column = lax.switch(pivot % 8, [along_y(k) for k in range(8)], diag, column)
    diag = diag + swap_cores(diag)
    mine = jnp.concatenate([column, strip])
    mine, diag = lax.optimization_barrier((mine, diag))
    theirs = swap_cores(mine)

    factor, inverse = factorize(diag)
    place = jnp.stack([pivot, my_row, my_col])
    trailing, panel_rows = update(
        place, factor, inverse, mine, theirs, flat, rows_here, row_count, col_count
    )
    return trailing.reshape(matrix.shape), panel_rows


def solution(mesh):
    placed = (P(None, "row", None, "col"), P())
    return jax.shard_map(
        on_device,
        mesh=mesh,
        in_specs=placed,
        out_specs=(P(None, "row", None, "col"), P(None, "row", None)),
        check_vma=False,
    )
```

```python
import functools

import jax
import jax.numpy as jnp
from jax import lax
from jax.experimental import pallas as pl
from jax.experimental.pallas import tpu as pltpu
from jax.sharding import PartitionSpec as P

HIGHEST = lax.Precision.HIGHEST
AXES = ("row", "col")
X, Z, Y = 128, 16, 2
RING = 8
COUNT = 1024
TILE = 128
BLOCK = 16
CHUNK = 3


def swap_cores(value):
    return lax.ppermute(value, AXES, [(d, d ^ 1) for d in range(COUNT)])


def send(value, stride, source, step, core=None):
    same = [p for p in range(RING) if p % 2 == source % 2]
    if step == 0:
        moves = {source: source ^ 2, source ^ 4: source ^ 6}
    elif step == 1:
        held = same if core is not None else [p for p in same if p & 4 == source & 4]
        moves = {p: 6 - p if p % 2 == 0 else 8 - p for p in held}
    else:
        moves = {p: p ^ 1 for p in same}
    pairs = []
    for device in range(COUNT):
        place = device // stride % RING
        if place in moves and core in (None, device % 2):
            pairs.append((device, device + (moves[place] - place) * stride))
    return lax.ppermute(value, AXES, pairs)


def hop(value, stride, source, step, core=None):
    return value + send(value, stride, source, step, core)


def along_z(key):
    z, y, core = key, key // 2, key % 2

    def branch(strip, column):
        strip = swap_cores(strip)
        column = hop(column, Y, y, 0, core)
        for step in range(3):
            strip = hop(strip, Z, z, step)
        return lax.optimization_barrier((strip, column))

    return branch


def along_x(key):
    x, y, core = key // 4, key % 4 // 2, key % 2

    def branch(strip, column):
        column = hop(column, Y, y, 1, core)
        for step in range(3):
            strip = hop(strip, X, x, step)
        return lax.optimization_barrier((strip, column))

    return branch


def along_y(key):
    y, core = key // 2, key % 2

    def branch(diag, column):
        arrived = send(column, Y, y, 2, core)
        for step in range(3):
            diag = hop(diag, Y, y, step, 1 - core)
        diag = diag + swap_cores(diag)
        arrived, diag = lax.optimization_barrier((arrived, diag))
        return lax.optimization_barrier((diag, column + arrived))

    return branch


def cut_kernel(cols, place_ref, matrix_ref, strip_ref, column_ref):
    which, at_row, at_col = place_ref[0], place_ref[1] == 1, place_ref[2] == 1
    for k in range(cols):
        strip_ref[k] = jnp.where(at_row, matrix_ref[pl.ds(k, TILE, stride=cols), :], 0.0)
    for a in range(column_ref.shape[0]):
        rows = matrix_ref[pl.ds(a * TILE * cols + which, TILE, stride=cols), :]
        column_ref[a] = jnp.where(at_col, rows, 0.0)


def cut(place, matrix, tiles, cols):
    vmem = pl.BlockSpec(memory_space=pltpu.VMEM)
    return pl.pallas_call(
        functools.partial(cut_kernel, cols),
        out_shape=(
            jax.ShapeDtypeStruct((cols, TILE, TILE), jnp.float32),
            jax.ShapeDtypeStruct((tiles, TILE, TILE), jnp.float32),
        ),
        in_specs=[pl.BlockSpec(memory_space=pltpu.SMEM), vmem],
        out_specs=(vmem, vmem),
        compiler_params=pltpu.CompilerParams(vmem_limit_bytes=16 * 2**20),
    )(place, matrix)


def row_of(value, row):
    return jnp.broadcast_to(value[row : row + 1, :], value.shape)


def factor_kernel(diag_ref, factor_ref, inverse_ref, left_ref, right_ref):
    sub = lax.broadcasted_iota(jnp.int32, (BLOCK, TILE), 0)
    lane = lax.broadcasted_iota(jnp.int32, (TILE, TILE), 1)
    row = lax.broadcasted_iota(jnp.int32, (TILE, TILE), 0)
    left_ref[...] = diag_ref[...]
    right_ref[...] = jnp.where(lane == row, 1.0, 0.0)
    for start in range(0, TILE, BLOCK):
        stop = start + BLOCK
        rows = pl.ds(start, BLOCK)
        left, right = left_ref[rows, :], right_ref[rows, :]
        cols = [jnp.broadcast_to(left[:, i : i + 1], (BLOCK, TILE)) for i in range(start, stop)]
        pivots = jnp.ones((BLOCK, TILE), jnp.float32)
        for j in range(BLOCK):
            pivot = row_of(cols[j], j)
            pivots = jnp.where(sub == j, pivot, pivots)
            scale = jnp.where(sub > j, cols[j], 0.0) * (1.0 / pivot)
            for i in range(j + 1, BLOCK):
                cols[i] = cols[i] - scale * row_of(cols[i], j)
            left = left - scale * row_of(left, j)
            right = right - scale * row_of(right, j)
        root = lax.rsqrt(pivots)
        root = root * (1.5 - 0.5 * pivots * root * root)
        left, right = left * root, right * root
        left_ref[rows, :] = left
        right_ref[rows, :] = right
        if stop < TILE:
            rest = pl.ds(stop, TILE - stop)
            step = lax.dot_general(
                left[:, stop:], jnp.concatenate([left, right], axis=1), (((0,), (0,)), ((), ())),
                precision=HIGHEST, preferred_element_type=jnp.float32,
            )
            left_ref[rest, :] = left_ref[rest, :] - step[:, :TILE]
            right_ref[rest, :] = right_ref[rest, :] - step[:, TILE:]
    factor_ref[...] = jnp.where(lane <= row, left_ref[...].T, 0.0)
    inverse_ref[...] = jnp.where(lane <= row, right_ref[...], 0.0)


def factorize(diag):
    shape = jax.ShapeDtypeStruct((TILE, TILE), jnp.float32)
    spec = pl.BlockSpec(memory_space=pltpu.VMEM)
    return pl.pallas_call(
        factor_kernel,
        out_shape=(shape, shape),
        in_specs=[spec],
        out_specs=(spec, spec),
        scratch_shapes=[pltpu.VMEM((TILE, TILE), jnp.float32)] * 2,
        compiler_params=pltpu.CompilerParams(vmem_limit_bytes=4 * 2**20),
    )(diag)


def update_kernel(
    row_count, col_count, place_ref, factor_ref, inverse_ref, mine_ref, theirs_ref, matrix_ref, trailing_ref,
    panel_ref, out, solved, out_sems, solved_sems,
):
    tiles = solved.shape[0]
    cols = mine_ref.shape[0] - tiles
    pivot, my_row, my_col = place_ref[0], place_ref[1], place_ref[2]
    inverse = inverse_ref[...]
    strip = jnp.concatenate([theirs_ref[tiles + k] for k in range(cols)], axis=1)
    right = jnp.dot(inverse, strip, precision=HIGHEST, preferred_element_type=jnp.float32)
    copies = []
    for first in range(0, tiles, CHUNK):
        count = min(CHUNK, tiles - first)
        column = mine_ref[first : first + count] + theirs_ref[first : first + count]
        left = lax.dot_general(
            column.reshape(count * TILE, TILE), inverse, (((1,), (1,)), ((), ())), precision=HIGHEST,
            preferred_element_type=jnp.float32,
        )
        step = jnp.dot(left, right, precision=HIGHEST, preferred_element_type=jnp.float32)
        for a in range(first, first + count):
            is_pivot = a * row_count + my_row == pivot
            here = slice((a - first) * TILE, (a - first + 1) * TILE)
            solved[a] = jnp.where(is_pivot, factor_ref[...], left[here])
            for k in range(cols):
                zero = is_pivot | (k * col_count + my_col == pivot)
                rows = pl.ds(a * TILE * cols + k, TILE, stride=cols)
                kept = matrix_ref[rows, :] - step[here, k * TILE : (k + 1) * TILE]
                out[rows, :] = jnp.where(zero, 0.0, kept)
        chunk, block = pl.ds(first, count), pl.ds(first * TILE * cols, count * TILE * cols)
        copies.append(pltpu.make_async_copy(solved.at[chunk], panel_ref.at[chunk], solved_sems.at[first // CHUNK]))
        copies.append(pltpu.make_async_copy(out.at[block], trailing_ref.at[block], out_sems.at[first // CHUNK]))
        copies[-2].start()
        copies[-1].start()
    for copy in copies:
        copy.wait()


def update(place, factor, inverse, mine, theirs, matrix, tiles, row_count, col_count):
    vmem = pl.BlockSpec(memory_space=pltpu.VMEM)
    hbm = pl.BlockSpec(memory_space=pl.ANY)
    panel = jax.ShapeDtypeStruct((tiles, TILE, TILE), jnp.float32)
    return pl.pallas_call(
        functools.partial(update_kernel, row_count, col_count),
        out_shape=(jax.ShapeDtypeStruct(matrix.shape, jnp.float32), panel),
        in_specs=[pl.BlockSpec(memory_space=pltpu.SMEM)] + [vmem] * 5,
        out_specs=(hbm, hbm),
        scratch_shapes=[
            pltpu.VMEM(matrix.shape, jnp.float32),
            pltpu.VMEM(panel.shape, jnp.float32),
            pltpu.SemaphoreType.DMA((pl.cdiv(tiles, CHUNK),)),
            pltpu.SemaphoreType.DMA((pl.cdiv(tiles, CHUNK),)),
        ],
        compiler_params=pltpu.CompilerParams(vmem_limit_bytes=16 * 2**20),
    )(place, factor, inverse, mine, theirs, matrix)


def on_device(matrix, panel):
    rows_here, tile, cols_here, _ = matrix.shape
    row_count = lax.axis_size("row")
    col_count = lax.axis_size("col")
    my_row = lax.axis_index("row")
    my_col = lax.axis_index("col")
    pivot = panel[0]
    which = pivot // col_count
    at_row = my_row == pivot
    at_col = my_col == pivot % col_count

    flat = matrix.reshape(rows_here * tile * cols_here, tile)
    held = jnp.stack([which, at_row.astype(jnp.int32), at_col.astype(jnp.int32)])
    strip, column = cut(held, flat, rows_here, cols_here)
    strip, column = lax.switch(pivot % 8, [along_z(k) for k in range(8)], strip, column)
    strip, column = lax.switch(
        pivot // 8 * 4 + pivot % 4, [along_x(k) for k in range(16)], strip, column
    )
    crossed = my_col ^ 1 == pivot % col_count
    diag = jnp.where(crossed, lax.dynamic_index_in_dim(strip, which, 0, keepdims=False), 0.0)
    diag, column = lax.switch(pivot % 8, [along_y(k) for k in range(8)], diag, column)
    mine = jnp.concatenate([column, strip])
    mine, diag = lax.optimization_barrier((mine, diag))
    theirs = swap_cores(mine)

    factor, inverse = factorize(diag)
    place = jnp.stack([pivot, my_row, my_col])
    trailing, panel_rows = update(
        place, factor, inverse, mine, theirs, flat, rows_here, row_count, col_count
    )
    return trailing.reshape(matrix.shape), panel_rows


def solution(mesh):
    placed = (P(None, "row", None, "col"), P())
    return jax.shard_map(
        on_device,
        mesh=mesh,
        in_specs=placed,
        out_specs=(P(None, "row", None, "col"), P(None, "row", None)),
        check_vma=False,
    )
```

```python
import functools

import jax
import jax.numpy as jnp
from jax import lax
from jax.experimental import pallas as pl
from jax.experimental.pallas import tpu as pltpu
from jax.sharding import PartitionSpec as P

HIGHEST = lax.Precision.HIGHEST
AXES = ("row", "col")
X, Z, Y = 128, 16, 2
RING = 8
COUNT = 1024
TILE = 128
BLOCK = 16
CHUNK = 3


def swap_cores(value):
    return lax.ppermute(value, AXES, [(d, d ^ 1) for d in range(COUNT)])


def send(value, stride, source, step, core=None):
    same = [p for p in range(RING) if p % 2 == source % 2]
    if step == 0:
        moves = {source: source ^ 2, source ^ 4: source ^ 6}
    elif step == 1:
        held = same if core is not None else [p for p in same if p & 4 == source & 4]
        moves = {p: 6 - p if p % 2 == 0 else 8 - p for p in held}
    else:
        moves = {p: p ^ 1 for p in same}
    pairs = []
    for device in range(COUNT):
        place = device // stride % RING
        if place in moves and core in (None, device % 2):
            pairs.append((device, device + (moves[place] - place) * stride))
    return lax.ppermute(value, AXES, pairs)


def hop(value, stride, source, step, core=None):
    return value + send(value, stride, source, step, core)


def along_x(pivot):
    x, y, core = pivot // 8, pivot % 16 // 2, pivot % 2

    def branch(strip, column):
        strip = swap_cores(strip)
        column = hop(column, Y, y, 0, core)
        for step in range(3):
            strip = hop(strip, X, x, step)
        return lax.optimization_barrier((strip, column))

    return branch


def other_plane(key):
    y, core = key // 2, key % 2

    def branch(strip, column):
        return lax.optimization_barrier((strip, hop(column, Y, y, 0, core)))

    return branch


def along_z(key):
    z, y, core = key, key // 2, key % 2

    def branch(strip, column):
        column = hop(column, Y, y, 1, core)
        for step in range(3):
            strip = hop(strip, Z, z, step)
        return lax.optimization_barrier((strip, column))

    return branch


def along_y(key):
    y, core = key // 2, key % 2

    def branch(diag, column):
        arrived = send(column, Y, y, 2, core)
        for step in range(3):
            diag = hop(diag, Y, y, step, 1 - core)
        diag = diag + swap_cores(diag)
        arrived, diag = lax.optimization_barrier((arrived, diag))
        return lax.optimization_barrier((diag, column + arrived))

    return branch


def cut_kernel(cols, place_ref, matrix_ref, strip_ref, column_ref):
    which, at_row, at_col = place_ref[0], place_ref[1] == 1, place_ref[2] == 1
    for k in range(cols):
        strip_ref[k] = jnp.where(at_row, matrix_ref[pl.ds(k, TILE, stride=cols), :], 0.0)
    for a in range(column_ref.shape[0]):
        rows = matrix_ref[pl.ds(a * TILE * cols + which, TILE, stride=cols), :]
        column_ref[a] = jnp.where(at_col, rows, 0.0)


def cut(place, matrix, tiles, cols):
    vmem = pl.BlockSpec(memory_space=pltpu.VMEM)
    return pl.pallas_call(
        functools.partial(cut_kernel, cols),
        out_shape=(
            jax.ShapeDtypeStruct((cols, TILE, TILE), jnp.float32),
            jax.ShapeDtypeStruct((tiles, TILE, TILE), jnp.float32),
        ),
        in_specs=[pl.BlockSpec(memory_space=pltpu.SMEM), vmem],
        out_specs=(vmem, vmem),
        compiler_params=pltpu.CompilerParams(vmem_limit_bytes=16 * 2**20),
    )(place, matrix)


def row_of(value, row):
    return jnp.broadcast_to(value[row : row + 1, :], value.shape)


def factor_kernel(diag_ref, factor_ref, inverse_ref, left_ref, right_ref):
    sub = lax.broadcasted_iota(jnp.int32, (BLOCK, TILE), 0)
    lane = lax.broadcasted_iota(jnp.int32, (TILE, TILE), 1)
    row = lax.broadcasted_iota(jnp.int32, (TILE, TILE), 0)
    left_ref[...] = diag_ref[...]
    right_ref[...] = jnp.where(lane == row, 1.0, 0.0)
    for start in range(0, TILE, BLOCK):
        stop = start + BLOCK
        rows = pl.ds(start, BLOCK)
        left, right = left_ref[rows, :], right_ref[rows, :]
        cols = [jnp.broadcast_to(left[:, i : i + 1], (BLOCK, TILE)) for i in range(start, stop)]
        pivots = jnp.ones((BLOCK, TILE), jnp.float32)
        for j in range(BLOCK):
            pivot = row_of(cols[j], j)
            pivots = jnp.where(sub == j, pivot, pivots)
            scale = jnp.where(sub > j, cols[j], 0.0) * (1.0 / pivot)
            for i in range(j + 1, BLOCK):
                cols[i] = cols[i] - scale * row_of(cols[i], j)
            left = left - scale * row_of(left, j)
            right = right - scale * row_of(right, j)
        root = lax.rsqrt(pivots)
        root = root * (1.5 - 0.5 * pivots * root * root)
        left, right = left * root, right * root
        left_ref[rows, :] = left
        right_ref[rows, :] = right
        if stop < TILE:
            rest = pl.ds(stop, TILE - stop)
            step = lax.dot_general(
                left[:, stop:], jnp.concatenate([left, right], axis=1), (((0,), (0,)), ((), ())),
                precision=HIGHEST, preferred_element_type=jnp.float32,
            )
            left_ref[rest, :] = left_ref[rest, :] - step[:, :TILE]
            right_ref[rest, :] = right_ref[rest, :] - step[:, TILE:]
    factor_ref[...] = jnp.where(lane <= row, left_ref[...].T, 0.0)
    inverse_ref[...] = jnp.where(lane <= row, right_ref[...], 0.0)


def factorize(diag):
    shape = jax.ShapeDtypeStruct((TILE, TILE), jnp.float32)
    spec = pl.BlockSpec(memory_space=pltpu.VMEM)
    return pl.pallas_call(
        factor_kernel,
        out_shape=(shape, shape),
        in_specs=[spec],
        out_specs=(spec, spec),
        scratch_shapes=[pltpu.VMEM((TILE, TILE), jnp.float32)] * 2,
        compiler_params=pltpu.CompilerParams(vmem_limit_bytes=4 * 2**20),
    )(diag)


def update_kernel(
    row_count, col_count, place_ref, factor_ref, inverse_ref, mine_ref, theirs_ref, matrix_ref, trailing_ref,
    panel_ref, out, solved, out_sems, solved_sems,
):
    tiles = solved.shape[0]
    cols = mine_ref.shape[0] - tiles
    pivot, my_row, my_col = place_ref[0], place_ref[1], place_ref[2]
    inverse = inverse_ref[...]
    strip = jnp.concatenate([theirs_ref[tiles + k] for k in range(cols)], axis=1)
    right = jnp.dot(inverse, strip, precision=HIGHEST, preferred_element_type=jnp.float32)
    copies = []
    for first in range(0, tiles, CHUNK):
        count = min(CHUNK, tiles - first)
        column = mine_ref[first : first + count] + theirs_ref[first : first + count]
        left = lax.dot_general(
            column.reshape(count * TILE, TILE), inverse, (((1,), (1,)), ((), ())), precision=HIGHEST,
            preferred_element_type=jnp.float32,
        )
        step = jnp.dot(left, right, precision=HIGHEST, preferred_element_type=jnp.float32)
        for a in range(first, first + count):
            is_pivot = a * row_count + my_row == pivot
            here = slice((a - first) * TILE, (a - first + 1) * TILE)
            solved[a] = jnp.where(is_pivot, factor_ref[...], left[here])
            for k in range(cols):
                zero = is_pivot | (k * col_count + my_col == pivot)
                rows = pl.ds(a * TILE * cols + k, TILE, stride=cols)
                kept = matrix_ref[rows, :] - step[here, k * TILE : (k + 1) * TILE]
                out[rows, :] = jnp.where(zero, 0.0, kept)
        chunk, block = pl.ds(first, count), pl.ds(first * TILE * cols, count * TILE * cols)
        copies.append(pltpu.make_async_copy(solved.at[chunk], panel_ref.at[chunk], solved_sems.at[first // CHUNK]))
        copies.append(pltpu.make_async_copy(out.at[block], trailing_ref.at[block], out_sems.at[first // CHUNK]))
        copies[-2].start()
        copies[-1].start()
    for copy in copies:
        copy.wait()


def update(place, factor, inverse, mine, theirs, matrix, tiles, row_count, col_count):
    vmem = pl.BlockSpec(memory_space=pltpu.VMEM)
    hbm = pl.BlockSpec(memory_space=pl.ANY)
    panel = jax.ShapeDtypeStruct((tiles, TILE, TILE), jnp.float32)
    return pl.pallas_call(
        functools.partial(update_kernel, row_count, col_count),
        out_shape=(jax.ShapeDtypeStruct(matrix.shape, jnp.float32), panel),
        in_specs=[pl.BlockSpec(memory_space=pltpu.SMEM)] + [vmem] * 5,
        out_specs=(hbm, hbm),
        scratch_shapes=[
            pltpu.VMEM(matrix.shape, jnp.float32),
            pltpu.VMEM(panel.shape, jnp.float32),
            pltpu.SemaphoreType.DMA((pl.cdiv(tiles, CHUNK),)),
            pltpu.SemaphoreType.DMA((pl.cdiv(tiles, CHUNK),)),
        ],
        compiler_params=pltpu.CompilerParams(vmem_limit_bytes=16 * 2**20),
    )(place, factor, inverse, mine, theirs, matrix)


def on_device(matrix, panel):
    rows_here, tile, cols_here, _ = matrix.shape
    row_count = lax.axis_size("row")
    col_count = lax.axis_size("col")
    my_row = lax.axis_index("row")
    my_col = lax.axis_index("col")
    pivot = panel[0]
    which = pivot // col_count
    at_row = my_row == pivot
    at_col = my_col == pivot % col_count

    flat = matrix.reshape(rows_here * tile * cols_here, tile)
    held = jnp.stack([which, at_row.astype(jnp.int32), at_col.astype(jnp.int32)])
    strip, column = cut(held, flat, rows_here, cols_here)
    key = pivot % RING
    branches = [other_plane(k) for k in range(RING)] + [along_x(p) for p in range(cols_here * col_count)]
    in_plane = my_row % RING == key
    strip, column = lax.switch(jnp.where(in_plane, RING + pivot, key), branches, strip, column)
    strip, column = lax.switch(key, [along_z(k) for k in range(RING)], strip, column)
    crossed = my_col ^ 1 == pivot % col_count
    diag = jnp.where(crossed, lax.dynamic_index_in_dim(strip, which, 0, keepdims=False), 0.0)
    diag, column = lax.switch(key, [along_y(k) for k in range(RING)], diag, column)
    mine = jnp.concatenate([column, strip])
    mine, diag = lax.optimization_barrier((mine, diag))
    theirs = swap_cores(mine)

    factor, inverse = factorize(diag)
    place = jnp.stack([pivot, my_row, my_col])
    trailing, panel_rows = update(
        place, factor, inverse, mine, theirs, flat, rows_here, row_count, col_count
    )
    return trailing.reshape(matrix.shape), panel_rows


def solution(mesh):
    placed = (P(None, "row", None, "col"), P())
    return jax.shard_map(
        on_device,
        mesh=mesh,
        in_specs=placed,
        out_specs=(P(None, "row", None, "col"), P(None, "row", None)),
        check_vma=False,
    )
```

```python
import functools

import jax
import jax.numpy as jnp
from jax import lax
from jax.experimental import pallas as pl
from jax.experimental.pallas import tpu as pltpu
from jax.sharding import PartitionSpec as P

HIGHEST = lax.Precision.HIGHEST
AXES = ("row", "col")
X, Z, Y = 128, 16, 2
RING = 8
COUNT = 1024
TILE = 128
BLOCK = 16
CHUNK = 3


def swap_cores(value):
    return lax.ppermute(value, AXES, [(d, d ^ 1) for d in range(COUNT)])


def send(value, stride, source, step, core=None, cross=False):
    same = [p for p in range(RING) if p % 2 == source % 2]
    if step == 0:
        moves = {source: source ^ 2, source ^ 4: source ^ 6}
    elif step == 1:
        held = same if core is not None else [p for p in same if p & 4 == source & 4]
        moves = {p: 6 - p if p % 2 == 0 else 8 - p for p in held}
    else:
        moves = {p: p ^ 1 for p in same}
    pairs = []
    for device in range(COUNT):
        place = device // stride % RING
        if place in moves and core in (None, device % 2):
            pairs.append((device, (device + (moves[place] - place) * stride) ^ int(cross)))
    return lax.ppermute(value, AXES, pairs)


def hop(value, stride, source, step, core=None):
    return value + send(value, stride, source, step, core)


def along_x(pivot):
    x, y, core = pivot // 8, pivot % 16 // 2, pivot % 2

    def branch(strip, column):
        column = hop(column, Y, y, 0, core)
        strip = send(strip, X, x, 0, cross=True) + swap_cores(strip)
        for step in (1, 2):
            strip = hop(strip, X, x, step)
        return lax.optimization_barrier((strip, column))

    return branch


def other_plane(key):
    y, core = key // 2, key % 2

    def branch(strip, column):
        return lax.optimization_barrier((strip, hop(column, Y, y, 0, core)))

    return branch


def along_z(key):
    z, y, core = key, key // 2, key % 2

    def branch(strip, column):
        column = hop(column, Y, y, 1, core)
        for step in range(3):
            strip = hop(strip, Z, z, step)
        return lax.optimization_barrier((strip, column))

    return branch


def along_y(key):
    y, core = key // 2, key % 2

    def branch(diag, column):
        arrived = send(column, Y, y, 2, core)
        for step in range(3):
            diag = hop(diag, Y, y, step, 1 - core)
        diag = diag + swap_cores(diag)
        arrived, diag = lax.optimization_barrier((arrived, diag))
        return lax.optimization_barrier((diag, column + arrived))

    return branch


def cut_kernel(cols, place_ref, matrix_ref, strip_ref, column_ref):
    which, at_row, at_col = place_ref[0], place_ref[1] == 1, place_ref[2] == 1
    for k in range(cols):
        strip_ref[k] = jnp.where(at_row, matrix_ref[pl.ds(k, TILE, stride=cols), :], 0.0)
    for a in range(column_ref.shape[0]):
        rows = matrix_ref[pl.ds(a * TILE * cols + which, TILE, stride=cols), :]
        column_ref[a] = jnp.where(at_col, rows, 0.0)


def cut(place, matrix, tiles, cols):
    vmem = pl.BlockSpec(memory_space=pltpu.VMEM)
    return pl.pallas_call(
        functools.partial(cut_kernel, cols),
        out_shape=(
            jax.ShapeDtypeStruct((cols, TILE, TILE), jnp.float32),
            jax.ShapeDtypeStruct((tiles, TILE, TILE), jnp.float32),
        ),
        in_specs=[pl.BlockSpec(memory_space=pltpu.SMEM), vmem],
        out_specs=(vmem, vmem),
        compiler_params=pltpu.CompilerParams(vmem_limit_bytes=16 * 2**20),
    )(place, matrix)


def row_of(value, row):
    return jnp.broadcast_to(value[row : row + 1, :], value.shape)


def factor_kernel(diag_ref, factor_ref, inverse_ref, left_ref, right_ref):
    sub = lax.broadcasted_iota(jnp.int32, (BLOCK, TILE), 0)
    lane = lax.broadcasted_iota(jnp.int32, (TILE, TILE), 1)
    row = lax.broadcasted_iota(jnp.int32, (TILE, TILE), 0)
    left_ref[...] = diag_ref[...]
    right_ref[...] = jnp.where(lane == row, 1.0, 0.0)
    for start in range(0, TILE, BLOCK):
        stop = start + BLOCK
        rows = pl.ds(start, BLOCK)
        left, right = left_ref[rows, :], right_ref[rows, :]
        cols = [jnp.broadcast_to(left[:, i : i + 1], (BLOCK, TILE)) for i in range(start, stop)]
        pivots = jnp.ones((BLOCK, TILE), jnp.float32)
        for j in range(BLOCK):
            pivot = row_of(cols[j], j)
            pivots = jnp.where(sub == j, pivot, pivots)
            scale = jnp.where(sub > j, cols[j], 0.0) * (1.0 / pivot)
            for i in range(j + 1, BLOCK):
                cols[i] = cols[i] - scale * row_of(cols[i], j)
            left = left - scale * row_of(left, j)
            right = right - scale * row_of(right, j)
        root = lax.rsqrt(pivots)
        root = root * (1.5 - 0.5 * pivots * root * root)
        left, right = left * root, right * root
        left_ref[rows, :] = left
        right_ref[rows, :] = right
        if stop < TILE:
            rest = pl.ds(stop, TILE - stop)
            step = lax.dot_general(
                left[:, stop:], jnp.concatenate([left, right], axis=1), (((0,), (0,)), ((), ())),
                precision=HIGHEST, preferred_element_type=jnp.float32,
            )
            left_ref[rest, :] = left_ref[rest, :] - step[:, :TILE]
            right_ref[rest, :] = right_ref[rest, :] - step[:, TILE:]
    factor_ref[...] = jnp.where(lane <= row, left_ref[...].T, 0.0)
    inverse_ref[...] = jnp.where(lane <= row, right_ref[...], 0.0)


def factorize(diag):
    shape = jax.ShapeDtypeStruct((TILE, TILE), jnp.float32)
    spec = pl.BlockSpec(memory_space=pltpu.VMEM)
    return pl.pallas_call(
        factor_kernel,
        out_shape=(shape, shape),
        in_specs=[spec],
        out_specs=(spec, spec),
        scratch_shapes=[pltpu.VMEM((TILE, TILE), jnp.float32)] * 2,
        compiler_params=pltpu.CompilerParams(vmem_limit_bytes=4 * 2**20),
    )(diag)


def update_kernel(
    row_count, col_count, place_ref, factor_ref, inverse_ref, mine_ref, theirs_ref, matrix_ref, trailing_ref,
    panel_ref, out, solved, out_sems, solved_sems,
):
    tiles = solved.shape[0]
    cols = mine_ref.shape[0] - tiles
    pivot, my_row, my_col = place_ref[0], place_ref[1], place_ref[2]
    inverse = inverse_ref[...]
    strip = jnp.concatenate([theirs_ref[tiles + k] for k in range(cols)], axis=1)
    right = jnp.dot(inverse, strip, precision=HIGHEST, preferred_element_type=jnp.float32)
    copies = []
    for first in range(0, tiles, CHUNK):
        count = min(CHUNK, tiles - first)
        column = mine_ref[first : first + count] + theirs_ref[first : first + count]
        left = lax.dot_general(
            column.reshape(count * TILE, TILE), inverse, (((1,), (1,)), ((), ())), precision=HIGHEST,
            preferred_element_type=jnp.float32,
        )
        step = jnp.dot(left, right, precision=HIGHEST, preferred_element_type=jnp.float32)
        for a in range(first, first + count):
            is_pivot = a * row_count + my_row == pivot
            here = slice((a - first) * TILE, (a - first + 1) * TILE)
            solved[a] = jnp.where(is_pivot, factor_ref[...], left[here])
            for k in range(cols):
                zero = is_pivot | (k * col_count + my_col == pivot)
                rows = pl.ds(a * TILE * cols + k, TILE, stride=cols)
                kept = matrix_ref[rows, :] - step[here, k * TILE : (k + 1) * TILE]
                out[rows, :] = jnp.where(zero, 0.0, kept)
        chunk, block = pl.ds(first, count), pl.ds(first * TILE * cols, count * TILE * cols)
        copies.append(pltpu.make_async_copy(solved.at[chunk], panel_ref.at[chunk], solved_sems.at[first // CHUNK]))
        copies.append(pltpu.make_async_copy(out.at[block], trailing_ref.at[block], out_sems.at[first // CHUNK]))
        copies[-2].start()
        copies[-1].start()
    for copy in copies:
        copy.wait()


def update(place, factor, inverse, mine, theirs, matrix, tiles, row_count, col_count):
    vmem = pl.BlockSpec(memory_space=pltpu.VMEM)
    hbm = pl.BlockSpec(memory_space=pl.ANY)
    panel = jax.ShapeDtypeStruct((tiles, TILE, TILE), jnp.float32)
    return pl.pallas_call(
        functools.partial(update_kernel, row_count, col_count),
        out_shape=(jax.ShapeDtypeStruct(matrix.shape, jnp.float32), panel),
        in_specs=[pl.BlockSpec(memory_space=pltpu.SMEM)] + [vmem] * 5,
        out_specs=(hbm, hbm),
        scratch_shapes=[
            pltpu.VMEM(matrix.shape, jnp.float32),
            pltpu.VMEM(panel.shape, jnp.float32),
            pltpu.SemaphoreType.DMA((pl.cdiv(tiles, CHUNK),)),
            pltpu.SemaphoreType.DMA((pl.cdiv(tiles, CHUNK),)),
        ],
        compiler_params=pltpu.CompilerParams(vmem_limit_bytes=16 * 2**20),
    )(place, factor, inverse, mine, theirs, matrix)


def on_device(matrix, panel):
    rows_here, tile, cols_here, _ = matrix.shape
    row_count = lax.axis_size("row")
    col_count = lax.axis_size("col")
    my_row = lax.axis_index("row")
    my_col = lax.axis_index("col")
    pivot = panel[0]
    which = pivot // col_count
    at_row = my_row == pivot
    at_col = my_col == pivot % col_count

    flat = matrix.reshape(rows_here * tile * cols_here, tile)
    held = jnp.stack([which, at_row.astype(jnp.int32), at_col.astype(jnp.int32)])
    strip, column = cut(held, flat, rows_here, cols_here)
    key = pivot % RING
    branches = [other_plane(k) for k in range(RING)] + [along_x(p) for p in range(cols_here * col_count)]
    in_plane = my_row % RING == key
    strip, column = lax.switch(jnp.where(in_plane, RING + pivot, key), branches, strip, column)
    strip, column = lax.switch(key, [along_z(k) for k in range(RING)], strip, column)
    crossed = my_col ^ 1 == pivot % col_count
    diag = jnp.where(crossed, lax.dynamic_index_in_dim(strip, which, 0, keepdims=False), 0.0)
    diag, column = lax.switch(key, [along_y(k) for k in range(RING)], diag, column)
    mine = jnp.concatenate([column, strip])
    mine, diag = lax.optimization_barrier((mine, diag))
    theirs = swap_cores(mine)

    factor, inverse = factorize(diag)
    place = jnp.stack([pivot, my_row, my_col])
    trailing, panel_rows = update(
        place, factor, inverse, mine, theirs, flat, rows_here, row_count, col_count
    )
    return trailing.reshape(matrix.shape), panel_rows


def solution(mesh):
    placed = (P(None, "row", None, "col"), P())
    return jax.shard_map(
        on_device,
        mesh=mesh,
        in_specs=placed,
        out_specs=(P(None, "row", None, "col"), P(None, "row", None)),
        check_vma=False,
    )
```

```python
import functools

import jax
import jax.numpy as jnp
from jax import lax
from jax.experimental import pallas as pl
from jax.experimental.pallas import tpu as pltpu
from jax.sharding import PartitionSpec as P

HIGHEST = lax.Precision.HIGHEST
AXES = ("row", "col")
X, Z, Y = 128, 16, 2
RING = 8
COUNT = 1024
TILE = 128
BLOCK = 16
CHUNK = 3


def swap_cores(value):
    return lax.ppermute(value, AXES, [(d, d ^ 1) for d in range(COUNT)])


def send(value, stride, source, step, core=None, cross=False):
    same = [p for p in range(RING) if p % 2 == source % 2]
    if step == 0:
        moves = {source: source ^ 2, source ^ 4: source ^ 6}
    elif step == 1:
        held = same if core is not None else [p for p in same if p & 4 == source & 4]
        moves = {p: 6 - p if p % 2 == 0 else 8 - p for p in held}
    else:
        moves = {p: p ^ 1 for p in same}
    pairs = []
    for device in range(COUNT):
        place = device // stride % RING
        if place in moves and core in (None, device % 2):
            pairs.append((device, (device + (moves[place] - place) * stride) ^ int(cross)))
    return lax.ppermute(value, AXES, pairs)


def hop(value, stride, source, step, core=None):
    return value + send(value, stride, source, step, core)


def along_x(pivot):
    x, y, core = pivot // 8, pivot % 16 // 2, pivot % 2

    def branch(strip, column):
        column = hop(column, Y, y, 0, core)
        strip = send(strip, X, x, 0, cross=True) + swap_cores(strip)
        for step in (1, 2):
            strip = hop(strip, X, x, step)
        return lax.optimization_barrier((strip, column))

    return branch


def other_plane(key):
    y, core = key // 2, key % 2

    def branch(strip, column):
        return lax.optimization_barrier((strip, hop(column, Y, y, 0, core)))

    return branch


def along_z(key):
    z, y, core = key, key // 2, key % 2

    def branch(strip, column):
        column = hop(column, Y, y, 1, core)
        for step in range(3):
            strip = hop(strip, Z, z, step)
        return lax.optimization_barrier((strip, column))

    return branch


def along_y(key):
    y, core = key // 2, key % 2

    def branch(diag, column):
        arrived = send(column, Y, y, 2, core)
        for step in (0, 1):
            diag = hop(diag, Y, y, step, 1 - core)
        quads = [[4 * q, 4 * q + 1, 4 * q + 2, 4 * q + 3] for q in range(lax.axis_size("col") // 4)]
        diag = jnp.sum(lax.all_gather(diag, "col", axis_index_groups=quads), axis=0)
        arrived, diag = lax.optimization_barrier((arrived, diag))
        return lax.optimization_barrier((diag, column + arrived))

    return branch


def cut_kernel(cols, place_ref, matrix_ref, strip_ref, column_ref):
    which, at_row, at_col = place_ref[0], place_ref[1] == 1, place_ref[2] == 1
    for k in range(cols):
        strip_ref[k] = jnp.where(at_row, matrix_ref[pl.ds(k, TILE, stride=cols), :], 0.0)
    for a in range(column_ref.shape[0]):
        rows = matrix_ref[pl.ds(a * TILE * cols + which, TILE, stride=cols), :]
        column_ref[a] = jnp.where(at_col, rows, 0.0)


def cut(place, matrix, tiles, cols):
    vmem = pl.BlockSpec(memory_space=pltpu.VMEM)
    return pl.pallas_call(
        functools.partial(cut_kernel, cols),
        out_shape=(
            jax.ShapeDtypeStruct((cols, TILE, TILE), jnp.float32),
            jax.ShapeDtypeStruct((tiles, TILE, TILE), jnp.float32),
        ),
        in_specs=[pl.BlockSpec(memory_space=pltpu.SMEM), vmem],
        out_specs=(vmem, vmem),
        compiler_params=pltpu.CompilerParams(vmem_limit_bytes=16 * 2**20),
    )(place, matrix)


def row_of(value, row):
    return jnp.broadcast_to(value[row : row + 1, :], value.shape)


def factor_kernel(diag_ref, factor_ref, inverse_ref, left_ref, right_ref):
    sub = lax.broadcasted_iota(jnp.int32, (BLOCK, TILE), 0)
    lane = lax.broadcasted_iota(jnp.int32, (TILE, TILE), 1)
    row = lax.broadcasted_iota(jnp.int32, (TILE, TILE), 0)
    left_ref[...] = diag_ref[...]
    right_ref[...] = jnp.where(lane == row, 1.0, 0.0)
    for start in range(0, TILE, BLOCK):
        stop = start + BLOCK
        rows = pl.ds(start, BLOCK)
        left, right = left_ref[rows, :], right_ref[rows, :]
        cols = [jnp.broadcast_to(left[:, i : i + 1], (BLOCK, TILE)) for i in range(start, stop)]
        pivots = jnp.ones((BLOCK, TILE), jnp.float32)
        for j in range(BLOCK):
            pivot = row_of(cols[j], j)
            pivots = jnp.where(sub == j, pivot, pivots)
            scale = jnp.where(sub > j, cols[j], 0.0) * (1.0 / pivot)
            for i in range(j + 1, BLOCK):
                cols[i] = cols[i] - scale * row_of(cols[i], j)
            left = left - scale * row_of(left, j)
            right = right - scale * row_of(right, j)
        root = lax.rsqrt(pivots)
        root = root * (1.5 - 0.5 * pivots * root * root)
        left, right = left * root, right * root
        left_ref[rows, :] = left
        right_ref[rows, :] = right
        if stop < TILE:
            rest = pl.ds(stop, TILE - stop)
            step = lax.dot_general(
                left[:, stop:], jnp.concatenate([left, right], axis=1), (((0,), (0,)), ((), ())),
                precision=HIGHEST, preferred_element_type=jnp.float32,
            )
            left_ref[rest, :] = left_ref[rest, :] - step[:, :TILE]
            right_ref[rest, :] = right_ref[rest, :] - step[:, TILE:]
    factor_ref[...] = jnp.where(lane <= row, left_ref[...].T, 0.0)
    inverse_ref[...] = jnp.where(lane <= row, right_ref[...], 0.0)


def factorize(diag):
    shape = jax.ShapeDtypeStruct((TILE, TILE), jnp.float32)
    spec = pl.BlockSpec(memory_space=pltpu.VMEM)
    return pl.pallas_call(
        factor_kernel,
        out_shape=(shape, shape),
        in_specs=[spec],
        out_specs=(spec, spec),
        scratch_shapes=[pltpu.VMEM((TILE, TILE), jnp.float32)] * 2,
        compiler_params=pltpu.CompilerParams(vmem_limit_bytes=4 * 2**20),
    )(diag)


def update_kernel(
    row_count, col_count, place_ref, factor_ref, inverse_ref, mine_ref, theirs_ref, matrix_ref, trailing_ref,
    panel_ref, out, solved, out_sems, solved_sems,
):
    tiles = solved.shape[0]
    cols = mine_ref.shape[0] - tiles
    pivot, my_row, my_col = place_ref[0], place_ref[1], place_ref[2]
    inverse = inverse_ref[...]
    strip = jnp.concatenate([theirs_ref[tiles + k] for k in range(cols)], axis=1)
    right = jnp.dot(inverse, strip, precision=HIGHEST, preferred_element_type=jnp.float32)
    copies = []
    for first in range(0, tiles, CHUNK):
        count = min(CHUNK, tiles - first)
        column = mine_ref[first : first + count] + theirs_ref[first : first + count]
        left = lax.dot_general(
            column.reshape(count * TILE, TILE), inverse, (((1,), (1,)), ((), ())), precision=HIGHEST,
            preferred_element_type=jnp.float32,
        )
        step = jnp.dot(left, right, precision=HIGHEST, preferred_element_type=jnp.float32)
        for a in range(first, first + count):
            is_pivot = a * row_count + my_row == pivot
            here = slice((a - first) * TILE, (a - first + 1) * TILE)
            solved[a] = jnp.where(is_pivot, factor_ref[...], left[here])
            for k in range(cols):
                zero = is_pivot | (k * col_count + my_col == pivot)
                rows = pl.ds(a * TILE * cols + k, TILE, stride=cols)
                kept = matrix_ref[rows, :] - step[here, k * TILE : (k + 1) * TILE]
                out[rows, :] = jnp.where(zero, 0.0, kept)
        chunk, block = pl.ds(first, count), pl.ds(first * TILE * cols, count * TILE * cols)
        copies.append(pltpu.make_async_copy(solved.at[chunk], panel_ref.at[chunk], solved_sems.at[first // CHUNK]))
        copies.append(pltpu.make_async_copy(out.at[block], trailing_ref.at[block], out_sems.at[first // CHUNK]))
        copies[-2].start()
        copies[-1].start()
    for copy in copies:
        copy.wait()


def update(place, factor, inverse, mine, theirs, matrix, tiles, row_count, col_count):
    vmem = pl.BlockSpec(memory_space=pltpu.VMEM)
    hbm = pl.BlockSpec(memory_space=pl.ANY)
    panel = jax.ShapeDtypeStruct((tiles, TILE, TILE), jnp.float32)
    return pl.pallas_call(
        functools.partial(update_kernel, row_count, col_count),
        out_shape=(jax.ShapeDtypeStruct(matrix.shape, jnp.float32), panel),
        in_specs=[pl.BlockSpec(memory_space=pltpu.SMEM)] + [vmem] * 5,
        out_specs=(hbm, hbm),
        scratch_shapes=[
            pltpu.VMEM(matrix.shape, jnp.float32),
            pltpu.VMEM(panel.shape, jnp.float32),
            pltpu.SemaphoreType.DMA((pl.cdiv(tiles, CHUNK),)),
            pltpu.SemaphoreType.DMA((pl.cdiv(tiles, CHUNK),)),
        ],
        compiler_params=pltpu.CompilerParams(vmem_limit_bytes=16 * 2**20),
    )(place, factor, inverse, mine, theirs, matrix)


def on_device(matrix, panel):
    rows_here, tile, cols_here, _ = matrix.shape
    row_count = lax.axis_size("row")
    col_count = lax.axis_size("col")
    my_row = lax.axis_index("row")
    my_col = lax.axis_index("col")
    pivot = panel[0]
    which = pivot // col_count
    at_row = my_row == pivot
    at_col = my_col == pivot % col_count

    flat = matrix.reshape(rows_here * tile * cols_here, tile)
    held = jnp.stack([which, at_row.astype(jnp.int32), at_col.astype(jnp.int32)])
    strip, column = cut(held, flat, rows_here, cols_here)
    key = pivot % RING
    branches = [other_plane(k) for k in range(RING)] + [along_x(p) for p in range(cols_here * col_count)]
    in_plane = my_row % RING == key
    strip, column = lax.switch(jnp.where(in_plane, RING + pivot, key), branches, strip, column)
    strip, column = lax.switch(key, [along_z(k) for k in range(RING)], strip, column)
    crossed = my_col ^ 1 == pivot % col_count
    diag = jnp.where(crossed, lax.dynamic_index_in_dim(strip, which, 0, keepdims=False), 0.0)
    diag, column = lax.switch(key, [along_y(k) for k in range(RING)], diag, column)
    mine = jnp.concatenate([column, strip])
    mine, diag = lax.optimization_barrier((mine, diag))
    theirs = swap_cores(mine)

    factor, inverse = factorize(diag)
    place = jnp.stack([pivot, my_row, my_col])
    trailing, panel_rows = update(
        place, factor, inverse, mine, theirs, flat, rows_here, row_count, col_count
    )
    return trailing.reshape(matrix.shape), panel_rows


def solution(mesh):
    placed = (P(None, "row", None, "col"), P())
    return jax.shard_map(
        on_device,
        mesh=mesh,
        in_specs=placed,
        out_specs=(P(None, "row", None, "col"), P(None, "row", None)),
        check_vma=False,
    )
```

```python
import functools

import jax
import jax.numpy as jnp
from jax import lax
from jax.experimental import pallas as pl
from jax.experimental.pallas import tpu as pltpu
from jax.sharding import PartitionSpec as P

HIGHEST = lax.Precision.HIGHEST
AXES = ("row", "col")
X, Z, Y = 128, 16, 2
RING = 8
COUNT = 1024
TILE = 128
BLOCK = 16
CHUNK = 3


def swap_cores(value):
    return lax.ppermute(value, AXES, [(d, d ^ 1) for d in range(COUNT)])


def send(value, stride, source, step, core=None, cross=False):
    same = [p for p in range(RING) if p % 2 == source % 2]
    if step == 0:
        moves = {source: source ^ 2, source ^ 4: source ^ 6}
    elif step == 1:
        held = same if core is not None else [p for p in same if p & 4 == source & 4]
        moves = {p: 6 - p if p % 2 == 0 else 8 - p for p in held}
    else:
        moves = {p: p ^ 1 for p in same}
    pairs = []
    for device in range(COUNT):
        place = device // stride % RING
        if place in moves and core in (None, device % 2):
            pairs.append((device, (device + (moves[place] - place) * stride) ^ int(cross)))
    return lax.ppermute(value, AXES, pairs)


def hop(value, stride, source, step, core=None):
    return value + send(value, stride, source, step, core)


def along_x(pivot):
    x, y, core = pivot // 8, pivot % 16 // 2, pivot % 2

    def branch(strip, column):
        column = hop(column, Y, y, 0, core)
        strip = send(strip, X, x, 0, cross=True) + swap_cores(strip)
        for step in (1, 2):
            strip = hop(strip, X, x, step)
        return lax.optimization_barrier((strip, column))

    return branch


def other_plane(key):
    y, core = key // 2, key % 2

    def branch(strip, column):
        return lax.optimization_barrier((strip, hop(column, Y, y, 0, core)))

    return branch


def along_z(key):
    z, y, core = key, key // 2, key % 2

    def branch(strip, column):
        column = hop(column, Y, y, 1, core)
        for step in (0, 1):
            strip = hop(strip, Z, z, step)
        pairs = [[2 * q, 2 * q + 1] for q in range(lax.axis_size("row") // 2)]
        strip = jnp.sum(lax.all_gather(strip, "row", axis_index_groups=pairs), axis=0)
        return lax.optimization_barrier((strip, column))

    return branch


def along_y(key):
    y, core = key // 2, key % 2

    def branch(diag, column):
        arrived = send(column, Y, y, 2, core)
        for step in (0, 1):
            diag = hop(diag, Y, y, step, 1 - core)
        quads = [[4 * q, 4 * q + 1, 4 * q + 2, 4 * q + 3] for q in range(lax.axis_size("col") // 4)]
        diag = jnp.sum(lax.all_gather(diag, "col", axis_index_groups=quads), axis=0)
        arrived, diag = lax.optimization_barrier((arrived, diag))
        return lax.optimization_barrier((diag, column + arrived))

    return branch


def cut_kernel(cols, place_ref, matrix_ref, strip_ref, column_ref):
    which, at_row, at_col = place_ref[0], place_ref[1] == 1, place_ref[2] == 1
    for k in range(cols):
        strip_ref[k] = jnp.where(at_row, matrix_ref[pl.ds(k, TILE, stride=cols), :], 0.0)
    for a in range(column_ref.shape[0]):
        rows = matrix_ref[pl.ds(a * TILE * cols + which, TILE, stride=cols), :]
        column_ref[a] = jnp.where(at_col, rows, 0.0)


def cut(place, matrix, tiles, cols):
    vmem = pl.BlockSpec(memory_space=pltpu.VMEM)
    return pl.pallas_call(
        functools.partial(cut_kernel, cols),
        out_shape=(
            jax.ShapeDtypeStruct((cols, TILE, TILE), jnp.float32),
            jax.ShapeDtypeStruct((tiles, TILE, TILE), jnp.float32),
        ),
        in_specs=[pl.BlockSpec(memory_space=pltpu.SMEM), vmem],
        out_specs=(vmem, vmem),
        compiler_params=pltpu.CompilerParams(vmem_limit_bytes=16 * 2**20),
    )(place, matrix)


def row_of(value, row):
    return jnp.broadcast_to(value[row : row + 1, :], value.shape)


def factor_kernel(diag_ref, factor_ref, inverse_ref, left_ref, right_ref):
    sub = lax.broadcasted_iota(jnp.int32, (BLOCK, TILE), 0)
    lane = lax.broadcasted_iota(jnp.int32, (TILE, TILE), 1)
    row = lax.broadcasted_iota(jnp.int32, (TILE, TILE), 0)
    left_ref[...] = diag_ref[...]
    right_ref[...] = jnp.where(lane == row, 1.0, 0.0)
    for start in range(0, TILE, BLOCK):
        stop = start + BLOCK
        rows = pl.ds(start, BLOCK)
        left, right = left_ref[rows, :], right_ref[rows, :]
        cols = [jnp.broadcast_to(left[:, i : i + 1], (BLOCK, TILE)) for i in range(start, stop)]
        pivots = jnp.ones((BLOCK, TILE), jnp.float32)
        for j in range(BLOCK):
            pivot = row_of(cols[j], j)
            pivots = jnp.where(sub == j, pivot, pivots)
            scale = jnp.where(sub > j, cols[j], 0.0) * (1.0 / pivot)
            for i in range(j + 1, BLOCK):
                cols[i] = cols[i] - scale * row_of(cols[i], j)
            left = left - scale * row_of(left, j)
            right = right - scale * row_of(right, j)
        root = lax.rsqrt(pivots)
        root = root * (1.5 - 0.5 * pivots * root * root)
        left, right = left * root, right * root
        left_ref[rows, :] = left
        right_ref[rows, :] = right
        if stop < TILE:
            rest = pl.ds(stop, TILE - stop)
            step = lax.dot_general(
                left[:, stop:], jnp.concatenate([left, right], axis=1), (((0,), (0,)), ((), ())),
                precision=HIGHEST, preferred_element_type=jnp.float32,
            )
            left_ref[rest, :] = left_ref[rest, :] - step[:, :TILE]
            right_ref[rest, :] = right_ref[rest, :] - step[:, TILE:]
    factor_ref[...] = jnp.where(lane <= row, left_ref[...].T, 0.0)
    inverse_ref[...] = jnp.where(lane <= row, right_ref[...], 0.0)


def factorize(diag):
    shape = jax.ShapeDtypeStruct((TILE, TILE), jnp.float32)
    spec = pl.BlockSpec(memory_space=pltpu.VMEM)
    return pl.pallas_call(
        factor_kernel,
        out_shape=(shape, shape),
        in_specs=[spec],
        out_specs=(spec, spec),
        scratch_shapes=[pltpu.VMEM((TILE, TILE), jnp.float32)] * 2,
        compiler_params=pltpu.CompilerParams(vmem_limit_bytes=4 * 2**20),
    )(diag)


def update_kernel(
    row_count, col_count, place_ref, factor_ref, inverse_ref, mine_ref, theirs_ref, matrix_ref, trailing_ref,
    panel_ref, out, solved, out_sems, solved_sems,
):
    tiles = solved.shape[0]
    cols = mine_ref.shape[0] - tiles
    pivot, my_row, my_col = place_ref[0], place_ref[1], place_ref[2]
    inverse = inverse_ref[...]
    strip = jnp.concatenate([theirs_ref[tiles + k] for k in range(cols)], axis=1)
    right = jnp.dot(inverse, strip, precision=HIGHEST, preferred_element_type=jnp.float32)
    copies = []
    for first in range(0, tiles, CHUNK):
        count = min(CHUNK, tiles - first)
        column = mine_ref[first : first + count] + theirs_ref[first : first + count]
        left = lax.dot_general(
            column.reshape(count * TILE, TILE), inverse, (((1,), (1,)), ((), ())), precision=HIGHEST,
            preferred_element_type=jnp.float32,
        )
        step = jnp.dot(left, right, precision=HIGHEST, preferred_element_type=jnp.float32)
        for a in range(first, first + count):
            is_pivot = a * row_count + my_row == pivot
            here = slice((a - first) * TILE, (a - first + 1) * TILE)
            solved[a] = jnp.where(is_pivot, factor_ref[...], left[here])
            for k in range(cols):
                zero = is_pivot | (k * col_count + my_col == pivot)
                rows = pl.ds(a * TILE * cols + k, TILE, stride=cols)
                kept = matrix_ref[rows, :] - step[here, k * TILE : (k + 1) * TILE]
                out[rows, :] = jnp.where(zero, 0.0, kept)
        chunk, block = pl.ds(first, count), pl.ds(first * TILE * cols, count * TILE * cols)
        copies.append(pltpu.make_async_copy(solved.at[chunk], panel_ref.at[chunk], solved_sems.at[first // CHUNK]))
        copies.append(pltpu.make_async_copy(out.at[block], trailing_ref.at[block], out_sems.at[first // CHUNK]))
        copies[-2].start()
        copies[-1].start()
    for copy in copies:
        copy.wait()


def update(place, factor, inverse, mine, theirs, matrix, tiles, row_count, col_count):
    vmem = pl.BlockSpec(memory_space=pltpu.VMEM)
    hbm = pl.BlockSpec(memory_space=pl.ANY)
    panel = jax.ShapeDtypeStruct((tiles, TILE, TILE), jnp.float32)
    return pl.pallas_call(
        functools.partial(update_kernel, row_count, col_count),
        out_shape=(jax.ShapeDtypeStruct(matrix.shape, jnp.float32), panel),
        in_specs=[pl.BlockSpec(memory_space=pltpu.SMEM)] + [vmem] * 5,
        out_specs=(hbm, hbm),
        scratch_shapes=[
            pltpu.VMEM(matrix.shape, jnp.float32),
            pltpu.VMEM(panel.shape, jnp.float32),
            pltpu.SemaphoreType.DMA((pl.cdiv(tiles, CHUNK),)),
            pltpu.SemaphoreType.DMA((pl.cdiv(tiles, CHUNK),)),
        ],
        compiler_params=pltpu.CompilerParams(vmem_limit_bytes=16 * 2**20),
    )(place, factor, inverse, mine, theirs, matrix)


def on_device(matrix, panel):
    rows_here, tile, cols_here, _ = matrix.shape
    row_count = lax.axis_size("row")
    col_count = lax.axis_size("col")
    my_row = lax.axis_index("row")
    my_col = lax.axis_index("col")
    pivot = panel[0]
    which = pivot // col_count
    at_row = my_row == pivot
    at_col = my_col == pivot % col_count

    flat = matrix.reshape(rows_here * tile * cols_here, tile)
    held = jnp.stack([which, at_row.astype(jnp.int32), at_col.astype(jnp.int32)])
    strip, column = cut(held, flat, rows_here, cols_here)
    key = pivot % RING
    branches = [other_plane(k) for k in range(RING)] + [along_x(p) for p in range(cols_here * col_count)]
    in_plane = my_row % RING == key
    strip, column = lax.switch(jnp.where(in_plane, RING + pivot, key), branches, strip, column)
    strip, column = lax.switch(key, [along_z(k) for k in range(RING)], strip, column)
    crossed = my_col ^ 1 == pivot % col_count
    diag = jnp.where(crossed, lax.dynamic_index_in_dim(strip, which, 0, keepdims=False), 0.0)
    diag, column = lax.switch(key, [along_y(k) for k in range(RING)], diag, column)
    mine = jnp.concatenate([column, strip])
    mine, diag = lax.optimization_barrier((mine, diag))
    theirs = swap_cores(mine)

    factor, inverse = factorize(diag)
    place = jnp.stack([pivot, my_row, my_col])
    trailing, panel_rows = update(
        place, factor, inverse, mine, theirs, flat, rows_here, row_count, col_count
    )
    return trailing.reshape(matrix.shape), panel_rows


def solution(mesh):
    placed = (P(None, "row", None, "col"), P())
    return jax.shard_map(
        on_device,
        mesh=mesh,
        in_specs=placed,
        out_specs=(P(None, "row", None, "col"), P(None, "row", None)),
        check_vma=False,
    )
```
